32 devices in a mesh: group: 16 (over z, y, core), mp: 2 (over x).
Axes of the slice: x: 2, y: 2, z: 4, core: 2. Of those that a mesh axis runs over, the one named last changes fastest.
Arguments:
- anchor: float32 [16, 2048, 2048], P(None, 'group', 'mp'), may hold values from -6 to 6
- momentum: float32 [16, 2048, 2048], P(None, 'group', 'mp'), may hold values from -3 to 3
- deltas: float32 [16, 2, 2048, 2048], P('group', None, None, 'mp'), may hold values from -3 to 3
- old_path: int32 [16, 2], replicated, may hold values from 0 to 7, as said below
- new_path: int32 [16, 2], replicated, may hold values from 0 to 7, as said below
- tokens: bfloat16 [16, 1024, 2048], P('group', None, 'mp'), may hold values from -40 to 40
- cotangent: bfloat16 [16, 1024, 2048], P('group', None, 'mp'), may hold values from -6 to 6
Outputs:
- new_anchor: float32 [16, 2048, 2048], P(None, 'group', 'mp')
- new_momentum: float32 [16, 2048, 2048], P(None, 'group', 'mp')
- grads: bfloat16 [16, 2, 2048, 2048], P('group', None, None, 'mp')
The draws below stay inside these ranges and needn't reach their ends.
Inputs may be any that keep to these rules, and one draw needn't show every extreme that they name: `old_path`: for each of the 2 levels, every one of the 8 modules is named by at least one group. `new_path`: for each of the 2 levels, every one of the 8 modules is named by at least one group.
All inputs are finite; a program needn't handle non-finite values.
Results may differ from the reference program's by a relative error of at most 0.014.
Values may be sent and summed in bfloat16 or wider, within the bound.
No kernel may reach another device: no remote copies, remote signals or barrier semaphores. Data moves between devices by JAX's collectives and lax.ppermute only.
A program may use at most 192 MiB of HBM per device.

```python
import math
import jax
import jax.numpy as jnp
from jax import lax

D = 2048
MODS = 8
LEVELS = 2
ROWS = 1024
GROUPS = 16
MODULES = 16
N_MP = 2


def path_table(key):
    columns = []
    for level in range(LEVELS):
        level_key = jax.random.fold_in(key, level)
        first_key, second_key, third_key, label_key, order_key = jax.random.split(level_key, 5)
        first = jax.random.randint(first_key, (GROUPS,), 0, MODS)
        second = jax.random.randint(second_key, (GROUPS,), 0, MODS)
        third = jax.random.randint(third_key, (GROUPS,), 0, MODS)
        skewed = jnp.minimum(jnp.minimum(first, second), third)
        positions = jnp.arange(GROUPS, dtype=jnp.int32)
        base = jnp.where(positions < MODS, positions, skewed)
        labels = jax.random.permutation(label_key, MODS)
        order = jax.random.permutation(order_key, GROUPS)
        columns.append(labels[base][order])
    return jnp.stack(columns, axis=1).astype(jnp.int32)


def draw_old_path(key, part):
    return path_table(jax.random.fold_in(key, 11))


def draw_new_path(key, part):
    return path_table(jax.random.fold_in(key, 23))


def draw_tokens(key, part):
    base_key, rough_key = jax.random.split(jax.random.fold_in(key, 37), 2)
    rough = jax.random.uniform(rough_key, (D,), jnp.float32, 0.7, 1.4)
    ramp = jnp.exp(jnp.linspace(math.log(0.2), math.log(2.0), D)).astype(jnp.float32)
    base = jnp.clip(jax.random.normal(base_key, (GROUPS, ROWS, D), jnp.float32), -4.5, 4.5)
    values = base * ramp * rough
    return values.astype(jnp.bfloat16)


def with_spikes(entries, stream_key, source, target, blocks, factor):
    owner, partner = [(jnp.arange(entries.shape[axis_at]) // (entries.shape[axis_at] // blocks)).reshape([-1 if axis == axis_at else 1 for axis in range(entries.ndim)]) for axis_at in (source, target)]
    chosen = jax.random.permutation(stream_key, blocks)[partner]
    strong = (owner == chosen) | (owner == (partner + blocks // 2) % blocks)
    return jnp.where(strong, factor * entries, entries)


def steps_of(rng, shape, cuts, smallest, top_value):
    def one(position, parts):
        draws = jax.random.uniform(jax.random.fold_in(jax.random.fold_in(rng, 6), position), (parts,), jnp.float32, smallest / len(cuts), top_value / len(cuts))
        return jnp.repeat(jnp.exp(draws), shape[position] // parts).reshape((-1,) + (1,) * (len(shape) - position - 1))

    loudness = one(*cuts[0])
    for cut in cuts[1:]:
        loudness = loudness * one(*cut)
    return loudness


def noise(stream_key, shape, width, most, pieces=(), kind=jnp.bfloat16):
    array = jax.random.normal(stream_key, shape, jnp.float32) * width
    if len(pieces) > 0:
        array = steps_of(stream_key, shape, pieces, -0.22, 0.18) * array
    return jnp.clip(array, min=-most, max=most).astype(kind)


def heavy_noise(key, shape, spread, reach, shards, heavy, held_as=jnp.bfloat16):
    values = spread * jax.random.normal(key, shape, jnp.float32)
    if shards:
        values = values * steps_of(key, shape, shards, -0.22, 0.18)
    return jnp.clip(with_spikes(values, jax.random.fold_in(key, 3), *heavy), -reach, reach).astype(held_as)


def setup_inputs(seed: int = 0) -> dict:
    seeds = jax.random.split(jax.random.key(seed), 8)
    anchor = noise(seeds[0], (MODULES, D, D), 1.0, 6.0, ((1, 16), (2, 2)), jnp.float32)
    momentum = noise(seeds[1], (MODULES, D, D), 0.5, 3.0, ((1, 16), (2, 2)), jnp.float32)
    deltas = heavy_noise(seeds[2], (GROUPS, LEVELS, D, D), 0.5, 3.0, ((0, 16), (3, 2)), (0, 2, 16, 2.0), jnp.float32)
    old_path = draw_old_path(jax.random.fold_in(seeds[7], 71), 0)
    new_path = draw_new_path(jax.random.fold_in(seeds[7], 71), 0)
    tokens = draw_tokens(jax.random.fold_in(seeds[7], 71), 0)
    cotangent = noise(seeds[6], (GROUPS, ROWS, D), 1.0, 6.0, ((0, 16), (2, 2)))
    return {"anchor": anchor, "momentum": momentum, "deltas": deltas, "old_path": old_path, "new_path": new_path, "tokens": tokens, "cotangent": cotangent}


outer_rate = 0.7
momentum_rate = 0.9
epsilon = 1e-06

def silu_slope(values):
    sigmoid_part = jax.nn.sigmoid(values)
    return sigmoid_part * (1.0 + values * (1.0 - sigmoid_part))

def normalize(hidden):
    mean_square = lax.optimization_barrier(jnp.mean(hidden * hidden, axis=-1))
    scale = lax.rsqrt(mean_square + epsilon)
    return ((hidden * scale[:, None]).astype(jnp.bfloat16), scale)

def reference(anchor, momentum, deltas, old_path, new_path, tokens, cotangent):
    factor = 1.0 / math.sqrt(D)
    level_offsets = jnp.arange(LEVELS, dtype=jnp.int32) * MODS
    old_index = (old_path + level_offsets[None, :]).astype(jnp.int32).reshape(-1)
    flat_deltas = deltas.reshape(GROUPS * LEVELS, D, D)
    sums = jax.ops.segment_sum(flat_deltas, old_index, num_segments=MODULES)
    counts = jax.ops.segment_sum(jnp.ones((GROUPS * LEVELS,), jnp.float32), old_index, num_segments=MODULES)
    outer_grad = sums / counts[:, None, None]
    new_momentum = momentum_rate * momentum + outer_grad
    new_anchor = anchor - outer_rate * (outer_grad + momentum_rate * new_momentum)
    new_index = (new_path + level_offsets[None, :]).astype(jnp.int32)

    def one_group(inputs):
        tokens_row, grad_row, index_row = inputs
        first_weight = lax.dynamic_index_in_dim(new_anchor, index_row[0], 0, keepdims=False).astype(jnp.bfloat16)
        second_weight = lax.dynamic_index_in_dim(new_anchor, index_row[1], 0, keepdims=False).astype(jnp.bfloat16)
        first_state = tokens_row.astype(jnp.float32)
        first_normed, first_scale = normalize(first_state)
        first_pre = jnp.dot(first_normed, first_weight, preferred_element_type=jnp.float32) * factor
        second_state = (first_state + jax.nn.silu(first_pre)).astype(jnp.bfloat16).astype(jnp.float32)
        second_normed, second_scale = normalize(second_state)
        second_pre = jnp.dot(second_normed, second_weight, preferred_element_type=jnp.float32) * factor
        upstream = grad_row.astype(jnp.float32)
        second_slope = (upstream * silu_slope(second_pre)).astype(jnp.bfloat16)
        second_grad = (lax.dot_general(second_normed, second_slope, (((0,), (0,)), ((), ())), preferred_element_type=jnp.float32) * factor).astype(jnp.bfloat16)
        slope_blocks = second_slope.astype(jnp.float32).reshape(ROWS, N_MP, D // N_MP)
        weight_blocks = second_weight.astype(jnp.float32).reshape(D, N_MP, D // N_MP)
        partial_terms = jnp.einsum('rpc,dpc->prd', slope_blocks, weight_blocks, precision=lax.Precision.HIGHEST) * factor
        rounded = lax.optimization_barrier(partial_terms.astype(jnp.bfloat16)).astype(jnp.float32)
        normed_grad = lax.optimization_barrier(jnp.sum(rounded, axis=0))
        inner = lax.optimization_barrier(jnp.sum(normed_grad * second_state, axis=-1))
        state_grad = upstream + second_scale[:, None] * normed_grad - second_state * (second_scale ** 3 * inner / D)[:, None]
        first_slope = (state_grad * silu_slope(first_pre)).astype(jnp.bfloat16)
        first_grad = (lax.dot_general(first_normed, first_slope, (((0,), (0,)), ((), ())), preferred_element_type=jnp.float32) * factor).astype(jnp.bfloat16)
        return jnp.stack([first_grad, second_grad])
    grads = lax.map(one_group, (tokens, cotangent, new_index))
    return (new_anchor, new_momentum, grads)
```

```python
import functools
import math

import jax
import jax.numpy as jnp
from jax import lax
from jax.experimental import pallas as pl
from jax.experimental.pallas import tpu as pltpu
from jax.sharding import PartitionSpec as P

outer_rate = 0.7
momentum_rate = 0.9
epsilon = 1e-06

VMEM = 60 * 1024 * 1024
TAIL_CHUNKS = 4

f32 = jnp.float32
bf16 = jnp.bfloat16


def params(**kw):
    return pltpu.CompilerParams(vmem_limit_bytes=VMEM, **kw)


def silu_slope(values):
    sigmoid_part = jax.nn.sigmoid(values)
    return sigmoid_part * (1.0 + values * (1.0 - sigmoid_part))


def cast_kernel(src, dst):
    dst[...] = src[...].reshape(dst.shape).astype(dst.dtype)


def cast_level(deltas, level, groups):
    _, _, depth, columns = deltas.shape
    rows = depth // groups
    per = 2 if groups % 2 == 0 else 1
    return pl.pallas_call(
        cast_kernel,
        grid=(groups // per,),
        in_specs=[pl.BlockSpec((1, 1, per * rows, columns), lambda i: (0, level, i, 0))],
        out_specs=pl.BlockSpec((per, rows, columns), lambda i: (i, 0, 0)),
        out_shape=jax.ShapeDtypeStruct((groups, rows, columns), bf16),
        compiler_params=params(),
        cost_estimate=pl.CostEstimate(
            flops=0, bytes_accessed=depth * columns * 6, transcendentals=0
        ),
    )(deltas)


def update_kernel(groups, mods, aliased, old, new, received, anchor, momentum, *rest):
    new_anchor, new_momentum, outgoing, total = rest[2:] if aliased else rest
    total[...] = jnp.zeros_like(total)
    for g in range(groups):
        m = old[g]
        total[m] = total[m] + received[g].astype(f32)
    for m in range(mods):
        count = jnp.int32(0)
        for g in range(groups):
            count = count + jnp.where(old[g] == m, 1, 0)
        outer_grad = total[m] / count.astype(f32)
        moved = momentum_rate * momentum[m] + outer_grad
        new_momentum[m] = moved
        total[m] = anchor[m] - outer_rate * (outer_grad + momentum_rate * moved)
        new_anchor[m] = total[m]
    for g in range(groups):
        outgoing[g] = total[new[g]].astype(outgoing.dtype)


def outer_update(received, anchor, momentum, old, new, level, levels, previous):
    groups, rows, columns = received.shape
    modules = anchor.shape[0]
    mods = modules // levels
    tile = 32 if rows % 32 == 0 else rows
    state = pl.BlockSpec((mods, tile, columns), lambda i, *_: (level, i, 0))
    block = pl.BlockSpec((groups, tile, columns), lambda i, *_: (0, i, 0))
    anywhere = pl.BlockSpec(memory_space=pl.ANY)
    aliased = previous is not None
    whole = jax.ShapeDtypeStruct(anchor.shape, f32)
    return pl.pallas_call(
        functools.partial(update_kernel, groups, mods, aliased),
        grid_spec=pltpu.PrefetchScalarGridSpec(
            num_scalar_prefetch=2,
            grid=(rows // tile,),
            in_specs=[block, state, state] + ([anywhere, anywhere] if aliased else []),
            out_specs=[state, state, block],
            scratch_shapes=[pltpu.VMEM((mods, tile, columns), f32)],
        ),
        out_shape=[whole, whole, jax.ShapeDtypeStruct(received.shape, bf16)],
        input_output_aliases={5: 0, 6: 1} if aliased else {},
        compiler_params=params(),
        cost_estimate=pl.CostEstimate(
            flops=0,
            bytes_accessed=rows * columns * (groups * 4 + mods * 16),
            transcendentals=0,
        ),
    )(old, new, received, anchor, momentum, *(previous or ()))


def grad_kernel(factor, aliased, normed, slope, *rest):
    out = rest[-1]
    product = lax.dot_general(
        normed[...], slope[...], (((0,), (0,)), ((), ())), preferred_element_type=f32
    )
    out[...] = (product * factor).astype(out.dtype).reshape(out.shape)


def level_grad(normed, slope, factor, level, levels, previous):
    rows, depth = normed.shape
    columns = slope.shape[1]
    tile = min(512, depth)
    aliased = previous is not None
    return pl.pallas_call(
        functools.partial(grad_kernel, factor, aliased),
        grid=(depth // tile,),
        in_specs=[
            pl.BlockSpec((rows, tile), lambda i: (0, i)),
            pl.BlockSpec((rows, columns), lambda i: (0, 0)),
        ]
        + ([pl.BlockSpec(memory_space=pl.ANY)] if aliased else []),
        out_specs=pl.BlockSpec((1, 1, tile, columns), lambda i: (0, level, i, 0)),
        out_shape=jax.ShapeDtypeStruct((1, levels, depth, columns), bf16),
        input_output_aliases={2: 0} if aliased else {},
        compiler_params=params(),
        cost_estimate=pl.CostEstimate(
            flops=2 * rows * depth * columns,
            bytes_accessed=2 * (rows * depth + rows * columns + depth * columns),
            transcendentals=0,
        ),
    )(normed, slope, *((previous,) if aliased else ()))


def gathered(own):
    return lax.all_gather(own, "mp", axis=1, tiled=True)


def normalize(whole):
    values = whole.astype(f32)
    scale = lax.rsqrt(jnp.mean(values * values, axis=-1, keepdims=True) + epsilon)
    return (values * scale).astype(bf16), scale


def shards(anchor, momentum, deltas, old_path, new_path, tokens, cotangent):
    groups = lax.axis_size("group")
    parts = lax.axis_size("mp")
    place = lax.axis_index("mp")
    levels = deltas.shape[1]
    depth = deltas.shape[2]
    columns = deltas.shape[3]
    factor = 1.0 / math.sqrt(depth)

    def exchange(blocks):
        return lax.all_to_all(blocks, "group", split_axis=0, concat_axis=0, tiled=True)

    received = [exchange(cast_level(deltas, level, groups)) for level in range(levels)]
    first_normed, _ = normalize(gathered(tokens[0]))

    previous = None
    loaded = []
    for level in range(levels):
        part_anchor, part_momentum, outgoing = outer_update(
            received[level],
            anchor,
            momentum,
            old_path[:, level],
            new_path[:, level],
            level,
            levels,
            previous,
        )
        previous = (part_anchor, part_momentum)
        loaded.append(exchange(outgoing).reshape(depth, columns))
    new_anchor, new_momentum = previous
    first_weight, second_weight = loaded

    first_state = tokens[0].astype(f32)
    upstream = cotangent[0].astype(f32)
    first_pre = jnp.dot(first_normed, first_weight, preferred_element_type=f32) * factor
    second_state = (first_state + jax.nn.silu(first_pre)).astype(bf16)
    second_normed, second_scale = normalize(gathered(second_state))

    rows = second_state.shape[0]
    run = rows // TAIL_CHUNKS
    own_features = depth // parts
    split_weight = second_weight.reshape(parts, own_features, columns)
    slopes, kept, arriving = [], [], []
    for r in range(TAIL_CHUNKS):
        here = slice(r * run, (r + 1) * run)
        pre = jnp.dot(second_normed[here], second_weight, preferred_element_type=f32) * factor
        slope = (upstream[here] * silu_slope(pre)).astype(bf16)
        dot = jnp.sum(slope.astype(f32) * pre, axis=-1)
        slopes.append((slope, dot))
        terms = []
        for step in range(parts):
            owner = lax.rem(place + step, parts)
            weight = lax.dynamic_index_in_dim(split_weight, owner, 0, keepdims=False)
            term = lax.dot_general(
                slope, weight, (((1,), (1,)), ((), ())), preferred_element_type=f32
            )
            terms.append((term * factor).astype(bf16))
        kept.append(terms[0])
        arriving.append(
            [
                lax.ppermute(
                    terms[step], "mp", [(p, (p + step) % parts) for p in range(parts)]
                )
                for step in range(1, parts)
            ]
        )
    inner = jnp.concatenate([dot for _, dot in slopes], axis=0)
    inner = lax.psum(inner, "mp")[:, None] / second_scale
    second_slope = jnp.concatenate([slope for slope, _ in slopes], axis=0)
    grads = level_grad(second_normed, second_slope, factor, 1, levels, None)
    first_slopes = []
    for r in range(TAIL_CHUNKS):
        here = slice(r * run, (r + 1) * run)
        normed_grad = kept[r].astype(f32)
        for term in arriving[r]:
            normed_grad = normed_grad + term.astype(f32)
        scale = second_scale[here]
        state_grad = (
            upstream[here]
            + scale * normed_grad
            - second_state[here].astype(f32) * (scale**3 * inner[here] / depth)
        )
        first_slopes.append((state_grad * silu_slope(first_pre[here])).astype(bf16))
    first_slope = jnp.concatenate(first_slopes, axis=0)
    grads = level_grad(first_normed, first_slope, factor, 0, levels, grads)
    return (new_anchor, new_momentum, grads)


def solution(mesh):
    in_specs = (
        P(None, "group", "mp"),
        P(None, "group", "mp"),
        P("group", None, None, "mp"),
        P(),
        P(),
        P("group", None, "mp"),
        P("group", None, "mp"),
    )
    out_specs = (P(None, "group", "mp"), P(None, "group", "mp"), P("group", None, None, "mp"))
    return jax.shard_map(shards, mesh=mesh, in_specs=in_specs, out_specs=out_specs, check_vma=False)
```

```python
import functools
import math

import jax
import jax.numpy as jnp
from jax import lax
from jax.experimental import pallas as pl
from jax.experimental.pallas import tpu as pltpu
from jax.sharding import PartitionSpec as P

outer_rate = 0.7
momentum_rate = 0.9
epsilon = 1e-06

MEBI = 1024 * 1024
RUN = 256
HALVES = 1
LIGHT = 16

f32 = jnp.float32
bf16 = jnp.bfloat16


def params(mebi=60):
    return pltpu.CompilerParams(vmem_limit_bytes=mebi * MEBI)


def silu_slope(values):
    sigmoid_part = jax.nn.sigmoid(values)
    return sigmoid_part * (1.0 + values * (1.0 - sigmoid_part))


def cast_kernel(src, dst):
    dst[...] = src[...].reshape(dst.shape).astype(dst.dtype)


def cast_level(deltas, level, groups):
    _, _, depth, columns = deltas.shape
    rows = depth // groups
    per = 4 if groups % 4 == 0 else 1
    return pl.pallas_call(
        cast_kernel,
        grid=(groups // per,),
        in_specs=[pl.BlockSpec((1, 1, per * rows, columns), lambda i: (0, level, i, 0))],
        out_specs=pl.BlockSpec((per, rows, columns), lambda i: (i, 0, 0)),
        out_shape=jax.ShapeDtypeStruct((groups, rows, columns), bf16),
        compiler_params=params(),
        cost_estimate=pl.CostEstimate(
            flops=0, bytes_accessed=depth * columns * 6, transcendentals=0
        ),
    )(deltas)


def update_kernel(groups, mods, aliased, old, new, received, anchor, momentum, *rest):
    new_anchor, new_momentum, outgoing, total = rest[2:] if aliased else rest
    total[...] = jnp.zeros_like(total)
    for g in range(groups):
        m = old[g]
        total[m] = total[m] + received[g].astype(f32)
    for m in range(mods):
        count = jnp.int32(0)
        for g in range(groups):
            count = count + jnp.where(old[g] == m, 1, 0)
        outer_grad = total[m] / count.astype(f32)
        moved = momentum_rate * momentum[m] + outer_grad
        new_momentum[m] = moved
        total[m] = anchor[m] - outer_rate * (outer_grad + momentum_rate * moved)
        new_anchor[m] = total[m]
    for g in range(groups):
        outgoing[g] = total[new[g]].astype(outgoing.dtype)


def outer_update(received, anchor, momentum, old, new, level, levels, previous):
    groups, rows, columns = received.shape
    modules = anchor.shape[0]
    mods = modules // levels
    tile = 32 if rows % 32 == 0 else rows
    state = pl.BlockSpec((mods, tile, columns), lambda i, *_: (level, i, 0))
    block = pl.BlockSpec((groups, tile, columns), lambda i, *_: (0, i, 0))
    anywhere = pl.BlockSpec(memory_space=pl.ANY)
    aliased = previous is not None
    whole = jax.ShapeDtypeStruct(anchor.shape, f32)
    return pl.pallas_call(
        functools.partial(update_kernel, groups, mods, aliased),
        grid_spec=pltpu.PrefetchScalarGridSpec(
            num_scalar_prefetch=2,
            grid=(rows // tile,),
            in_specs=[block, state, state] + ([anywhere, anywhere] if aliased else []),
            out_specs=[state, state, block],
            scratch_shapes=[pltpu.VMEM((mods, tile, columns), f32)],
        ),
        out_shape=[whole, whole, jax.ShapeDtypeStruct(received.shape, bf16)],
        input_output_aliases={5: 0, 6: 1} if aliased else {},
        compiler_params=params(),
        cost_estimate=pl.CostEstimate(
            flops=0,
            bytes_accessed=rows * columns * (groups * 4 + mods * 16),
            transcendentals=0,
        ),
    )(old, new, received, anchor, momentum, *(previous or ()))


OVER_ROWS = (((0,), (0,)), ((), ()))
OVER_COLUMNS = (((1,), (1,)), ((), ()))


def cost(flops, values, transcendentals=0):
    return pl.CostEstimate(flops=flops, bytes_accessed=values, transcendentals=transcendentals)


def norm_kernel(parts, depth, place, *refs):
    blocks = refs[:parts]
    out, scale = refs[parts : parts + 2]
    step = pl.program_id(1)

    @pl.when(step == 0)
    def _():
        total = jnp.zeros(scale.shape, f32)
        for block in blocks:
            values = block[...].astype(f32)
            total = total + jnp.sum(values * values, axis=-1, keepdims=True)
        scale[...] = lax.rsqrt(total / depth + epsilon)

    for at, block in enumerate(blocks):

        @pl.when(step == at)
        def _(block=block):
            out[...] = (block[...].astype(f32) * scale[...]).astype(out.dtype)


def normalize(own, parts, place):
    rows, width = own.shape
    depth = width * parts
    blocks = [own] + [lax.ppermute(own, "mp", around(parts, step)) for step in range(1, parts)]
    tile = min(256, rows)
    block = pl.BlockSpec((tile, width), lambda i, j, at: (i, 0))
    return pl.pallas_call(
        functools.partial(norm_kernel, parts, depth),
        grid_spec=pltpu.PrefetchScalarGridSpec(
            num_scalar_prefetch=1,
            grid=(rows // tile, parts),
            in_specs=[block] * parts,
            out_specs=[
                pl.BlockSpec(
                    (tile, width), lambda i, j, at: (i, lax.rem(at[0] + parts - j, parts))
                ),
                pl.BlockSpec((tile, 1), lambda i, j, at: (i, 0)),
            ],
        ),
        out_shape=[
            jax.ShapeDtypeStruct((rows, depth), bf16),
            jax.ShapeDtypeStruct((rows, 1), f32),
        ],
        compiler_params=params(),
        cost_estimate=cost(0, 4 * rows * depth),
    )(place.reshape(1).astype(jnp.int32), *blocks)


def grad_kernel(factor, normed, slope, out):
    product = lax.dot_general(normed[...], slope[...], OVER_ROWS, preferred_element_type=f32)
    out[...] = (product * factor).astype(out.dtype).reshape(out.shape)


def last_level_grad(normed, slope, factor, levels):
    rows, depth = normed.shape
    columns = slope.shape[1]
    tile = min(512, depth)
    return pl.pallas_call(
        functools.partial(grad_kernel, factor),
        grid=(depth // tile,),
        in_specs=[
            pl.BlockSpec((rows, tile), lambda i: (0, i)),
            pl.BlockSpec((rows, columns), lambda i: (0, 0)),
        ],
        out_specs=pl.BlockSpec((1, 1, tile, columns), lambda i: (0, levels - 1, i, 0)),
        out_shape=jax.ShapeDtypeStruct((1, levels, depth, columns), bf16),
        compiler_params=params(24),
        cost_estimate=cost(
            2 * rows * depth * columns // LIGHT,
            2 * (rows * depth + rows * columns + depth * columns) // LIGHT,
        ),
    )(normed, slope)


def state_kernel(factor, normed, weight, state, following, gate):
    pre = jnp.dot(normed[...], weight[...], preferred_element_type=f32) * factor
    sigmoid_part = jax.nn.sigmoid(pre)
    following[...] = (state[...].astype(f32) + pre * sigmoid_part).astype(bf16)
    gate[...] = sigmoid_part * (1.0 + pre * (1.0 - sigmoid_part))


def first_forward(normed, weight, state, factor):
    rows, depth = normed.shape
    columns = weight.shape[1]
    tile = min(256, rows)
    mine = pl.BlockSpec((tile, columns), lambda i: (i, 0))
    return pl.pallas_call(
        functools.partial(state_kernel, factor),
        grid=(rows // tile,),
        in_specs=[
            pl.BlockSpec((tile, depth), lambda i: (i, 0)),
            pl.BlockSpec((depth, columns), lambda i: (0, 0)),
            mine,
        ],
        out_specs=[mine, mine],
        out_shape=[
            jax.ShapeDtypeStruct((rows, columns), bf16),
            jax.ShapeDtypeStruct((rows, columns), f32),
        ],
        compiler_params=params(),
        cost_estimate=cost(
            2 * rows * depth * columns,
            2 * (rows * depth + 4 * rows * columns + depth * columns),
            rows * columns,
        ),
    )(normed, weight, state)


def slope_kernel(factor, width, at, normed, weight, upstream, *rest):
    slope, share, terms = rest[-3:]
    pre = jnp.dot(normed[...], weight[...], preferred_element_type=f32) * factor
    value = (upstream[...].astype(f32) * silu_slope(pre)).astype(bf16)
    slope[...] = value
    total = jnp.sum(value.astype(f32) * pre, axis=-1, keepdims=True)
    share[...] = jnp.broadcast_to(total, share.shape)
    start = pl.multiple_of(at[0] * width, width)
    product = lax.dot_general(
        value, weight[pl.ds(start, width), :], OVER_COLUMNS, preferred_element_type=f32
    )
    terms[...] = (product * factor).astype(terms.dtype)


def second_forward(normed, weight, upstream, where, width, factor, half, previous):
    rows, depth = normed.shape
    columns = weight.shape[1]
    tile = min(256, rows // HALVES)
    steps = rows // HALVES // tile
    first = half * steps
    mine = pl.BlockSpec((tile, columns), lambda i, at: (first + i, 0))
    return pl.pallas_call(
        functools.partial(slope_kernel, factor, width),
        grid_spec=pltpu.PrefetchScalarGridSpec(
            num_scalar_prefetch=1,
            grid=(steps,),
            in_specs=[
                pl.BlockSpec((tile, depth), lambda i, at: (first + i, 0)),
                pl.BlockSpec((depth, columns), lambda i, at: (0, 0)),
                mine,
            ]
            + [pl.BlockSpec(memory_space=pl.ANY)] * len(previous),
            out_specs=[
                mine,
                pl.BlockSpec((tile, 128), lambda i, at: (first + i, 0)),
                pl.BlockSpec((tile, width), lambda i, at: (i, 0)),
            ],
        ),
        out_shape=[
            jax.ShapeDtypeStruct((rows, columns), bf16),
            jax.ShapeDtypeStruct((rows, 128), f32),
            jax.ShapeDtypeStruct((rows // HALVES, width), bf16),
        ],
        input_output_aliases={4 + n: n for n in range(len(previous))},
        compiler_params=params(),
        cost_estimate=cost(
            2 * rows // HALVES * columns * (depth + width) // LIGHT,
            2 * (rows // HALVES * (depth + 2 * columns) + depth * columns) // LIGHT,
        ),
    )(where.reshape(1).astype(jnp.int32), normed, weight, upstream, *previous)


def term_kernel(factor, where, slope, weight, out):
    product = lax.dot_general(slope[...], weight[...], OVER_COLUMNS, preferred_element_type=f32)
    out[...] = (product * factor).astype(out.dtype)


def term(slope, weight, where, width, factor):
    rows, columns = slope.shape
    tile = min(512, rows)
    return pl.pallas_call(
        functools.partial(term_kernel, factor),
        grid_spec=pltpu.PrefetchScalarGridSpec(
            num_scalar_prefetch=1,
            grid=(rows // tile,),
            in_specs=[
                pl.BlockSpec((tile, columns), lambda i, at: (i, 0)),
                pl.BlockSpec((width, columns), lambda i, at: (at[0], 0)),
            ],
            out_specs=pl.BlockSpec((tile, width), lambda i, at: (i, 0)),
        ),
        out_shape=jax.ShapeDtypeStruct((rows, width), bf16),
        compiler_params=params(24),
        cost_estimate=cost(
            2 * rows * columns * width // LIGHT,
            2 * (rows * columns + columns * width + rows * width) // LIGHT,
        ),
    )(where.reshape(1).astype(jnp.int32), slope, weight)


def first_kernel(factor, cells, *refs):
    normed, scale, share, upstream, state, gate, kept = refs[:7]
    terms = refs[7:-3]
    out, slope = refs[-2:]
    count = len(terms) // len(cells)

    @pl.when(pl.program_id(0) == 0)
    def _():
        for number, (top, height, left, width) in enumerate(cells):
            span = slice(top, top + height)
            here = slice(left, left + width)
            normed_grad = kept[span, here].astype(f32)
            for other in terms[number * count : (number + 1) * count]:
                normed_grad = normed_grad + other[...].astype(f32)
            state_grad = (
                upstream[span, here].astype(f32)
                + scale[span, :] * normed_grad
                - state[span, here].astype(f32) * share[span, :]
            )
            slope[span, here] = (state_grad * gate[span, here]).astype(bf16)

    product = lax.dot_general(normed[...], slope[...], OVER_ROWS, preferred_element_type=f32)
    out[...] = (product * factor).astype(out.dtype).reshape(out.shape)


def first_level_grad(normed, scale, share, mine, cells, terms, block, width, factor, grads, mebi):
    rows, depth = normed.shape
    tile = min(512, depth)
    column = pl.BlockSpec((rows, 1), lambda i: (0, 0))
    part = pl.BlockSpec((rows, width), lambda i: (0, block))
    return pl.pallas_call(
        functools.partial(first_kernel, factor, cells),
        grid=(depth // tile,),
        in_specs=[pl.BlockSpec((rows, tile), lambda i: (0, i)), column, column]
        + [part] * len(mine)
        + [pl.BlockSpec(value.shape, lambda i: (0, 0)) for value in terms]
        + [pl.BlockSpec(memory_space=pl.ANY)],
        out_specs=pl.BlockSpec((1, 1, tile, width), lambda i: (0, 0, i, block)),
        out_shape=jax.ShapeDtypeStruct(grads.shape, bf16),
        scratch_shapes=[pltpu.VMEM((rows, width), bf16)],
        input_output_aliases={3 + len(mine) + len(terms): 0},
        compiler_params=params(mebi),
        cost_estimate=cost(
            2 * rows * depth * width // LIGHT,
            2 * (rows * depth + 7 * rows * width + depth * width) // LIGHT,
        ),
    )(normed, scale, share, *mine, *terms, grads)


def around(parts, step):
    return [(p, (p + step) % parts) for p in range(parts)]


def after(value, *others):
    return lax.optimization_barrier((value, *others))[0]


def shards(anchor, momentum, deltas, old_path, new_path, tokens, cotangent):
    groups = lax.axis_size("group")
    parts = lax.axis_size("mp")
    place = lax.axis_index("mp")
    levels = deltas.shape[1]
    depth = deltas.shape[2]
    columns = deltas.shape[3]
    factor = 1.0 / math.sqrt(depth)

    def exchange(blocks):
        return lax.all_to_all(blocks, "group", split_axis=0, concat_axis=0, tiled=True)

    received = [exchange(cast_level(deltas, level, groups)) for level in range(levels)]
    first_normed, _ = normalize(tokens[0], parts, place)
    received[0] = after(received[0], first_normed)

    previous = None
    loaded = []
    for level in range(levels):
        part_anchor, part_momentum, outgoing = outer_update(
            received[level],
            anchor,
            momentum,
            old_path[:, level],
            new_path[:, level],
            level,
            levels,
            previous,
        )
        previous = (part_anchor, part_momentum)
        loaded.append(exchange(outgoing).reshape(depth, columns))
    new_anchor, new_momentum = previous
    first_weight, second_weight = loaded

    upstream = cotangent[0]
    second_state, gate = first_forward(first_normed, first_weight, tokens[0], factor)
    second_normed, second_scale = normalize(second_state, parts, place)

    own_features = depth // parts
    width = min(RUN, own_features)
    runs = own_features // width

    def place_of(step, run):
        return lax.rem(place + step, parts) * runs + run

    def send(values):
        return [lax.ppermute(values[n], "mp", around(parts, n + 1)) for n in range(len(values))]

    def terms_of(source, run, steps):
        return [
            term(source, second_weight, place_of(step, run), width, factor) for step in steps
        ]

    rows = second_normed.shape[0]
    previous = ()
    leading = []
    for half in range(HALVES):
        slope, share, terms = second_forward(
            second_normed,
            second_weight,
            upstream,
            place_of(1, 0),
            width,
            factor,
            half,
            previous,
        )
        previous = (slope, share)
        leading.append(terms)
    own_share = share[:, 0].reshape(-1, 128)
    leading = [lax.ppermute(after(terms, own_share), "mp", around(parts, 1)) for terms in leading]
    share = own_share
    for other in send([own_share] * (parts - 1)):
        share = share + other
    sent = terms_of(slope, 0, range(2, parts))
    rest = [lax.ppermute(value, "mp", around(parts, n + 2)) for n, value in enumerate(sent)]
    height = rows // HALVES
    arrived = [[]]
    for half in range(HALVES):
        arrived[0].append(
            (
                half * height,
                height,
                [leading[half]] + [value[half * height : (half + 1) * height] for value in rest],
            )
        )
    last = slope
    source = slope
    for run in range(1, runs):
        if run == 3:
            kept = term(after(slope, last), second_weight, place, own_features, factor)
            source = after(slope, kept, *leading)
        sent = terms_of(source, run, range(1, parts))
        last = sent[0]
        arrived.append([(0, rows, send(sent))])
    if runs <= 3:
        kept = term(after(slope, last), second_weight, place, own_features, factor)
    grads = last_level_grad(second_normed, after(slope, last), factor, levels)
    scaled = second_scale**2 * after(share, grads).reshape(rows, 1) / depth
    mine = [upstream, second_state, gate, kept]
    bounds = [0, runs - 1, runs] if runs > 1 else [0, runs]
    for begin, end in zip(bounds[:-1], bounds[1:]):
        cells, terms = [], []
        for run in range(begin, end):
            for top, tall, values in arrived[run]:
                cells.append((top, tall, (run - begin) * width, width))
                terms += values
        grads = first_level_grad(
            first_normed,
            second_scale,
            scaled,
            mine,
            cells,
            terms,
            begin // (end - begin),
            (end - begin) * width,
            factor,
            grads,
            24 if end == runs else 40,
        )
    return (new_anchor, new_momentum, grads)


def solution(mesh):
    in_specs = (
        P(None, "group", "mp"),
        P(None, "group", "mp"),
        P("group", None, None, "mp"),
        P(),
        P(),
        P("group", None, "mp"),
        P("group", None, "mp"),
    )
    out_specs = (P(None, "group", "mp"), P(None, "group", "mp"), P("group", None, None, "mp"))
    return jax.shard_map(shards, mesh=mesh, in_specs=in_specs, out_specs=out_specs, check_vma=False)
```

```python
import functools
import math

import jax
import jax.numpy as jnp
from jax import lax
from jax.experimental import pallas as pl
from jax.experimental.pallas import tpu as pltpu
from jax.sharding import PartitionSpec as P

outer_rate = 0.7
momentum_rate = 0.9
epsilon = 1e-06

MEBI = 1024 * 1024
RUN = 256
LIGHT = 16
HEAVY = 4

f32 = jnp.float32
bf16 = jnp.bfloat16


def params(mebi=60):
    return pltpu.CompilerParams(vmem_limit_bytes=mebi * MEBI)


def silu_slope(values):
    sigmoid_part = jax.nn.sigmoid(values)
    return sigmoid_part * (1.0 + values * (1.0 - sigmoid_part))


def cast_kernel(src, dst):
    dst[...] = src[...].reshape(dst.shape).astype(dst.dtype)


def cast_level(deltas, level, groups):
    _, _, depth, columns = deltas.shape
    rows = depth // groups
    per = 4 if groups % 4 == 0 else 1
    return pl.pallas_call(
        cast_kernel,
        grid=(groups // per,),
        in_specs=[pl.BlockSpec((1, 1, per * rows, columns), lambda i: (0, level, i, 0))],
        out_specs=pl.BlockSpec((per, rows, columns), lambda i: (i, 0, 0)),
        out_shape=jax.ShapeDtypeStruct((groups, rows, columns), bf16),
        compiler_params=params(),
        cost_estimate=pl.CostEstimate(
            flops=0, bytes_accessed=depth * columns * 6, transcendentals=0
        ),
    )(deltas)


def update_kernel(groups, mods, aliased, old, new, received, anchor, momentum, *rest):
    new_anchor, new_momentum, outgoing, total = rest[2:] if aliased else rest
    total[...] = jnp.zeros_like(total)
    for g in range(groups):
        m = old[g]
        total[m] = total[m] + received[g].astype(f32)
    for m in range(mods):
        count = jnp.int32(0)
        for g in range(groups):
            count = count + jnp.where(old[g] == m, 1, 0)
        outer_grad = total[m] / count.astype(f32)
        moved = momentum_rate * momentum[m] + outer_grad
        new_momentum[m] = moved
        total[m] = anchor[m] - outer_rate * (outer_grad + momentum_rate * moved)
        new_anchor[m] = total[m]
    for g in range(groups):
        outgoing[g] = total[new[g]].astype(outgoing.dtype)


def outer_update(received, anchor, momentum, old, new, level, levels, previous):
    groups, rows, columns = received.shape
    modules = anchor.shape[0]
    mods = modules // levels
    tile = 32 if rows % 32 == 0 else rows
    state = pl.BlockSpec((mods, tile, columns), lambda i, *_: (level, i, 0))
    block = pl.BlockSpec((groups, tile, columns), lambda i, *_: (0, i, 0))
    anywhere = pl.BlockSpec(memory_space=pl.ANY)
    aliased = previous is not None
    whole = jax.ShapeDtypeStruct(anchor.shape, f32)
    return pl.pallas_call(
        functools.partial(update_kernel, groups, mods, aliased),
        grid_spec=pltpu.PrefetchScalarGridSpec(
            num_scalar_prefetch=2,
            grid=(rows // tile,),
            in_specs=[block, state, state] + ([anywhere, anywhere] if aliased else []),
            out_specs=[state, state, block],
            scratch_shapes=[pltpu.VMEM((mods, tile, columns), f32)],
        ),
        out_shape=[whole, whole, jax.ShapeDtypeStruct(received.shape, bf16)],
        input_output_aliases={5: 0, 6: 1} if aliased else {},
        compiler_params=params(),
        cost_estimate=pl.CostEstimate(
            flops=0,
            bytes_accessed=rows * columns * (groups * 4 + mods * 16),
            transcendentals=0,
        ),
    )(old, new, received, anchor, momentum, *(previous or ()))


OVER_ROWS = (((0,), (0,)), ((), ()))
OVER_COLUMNS = (((1,), (1,)), ((), ()))


def cost(flops, values, transcendentals=0):
    return pl.CostEstimate(flops=flops, bytes_accessed=values, transcendentals=transcendentals)


def norm_kernel(parts, depth, place, *refs):
    blocks = refs[:parts]
    out, scale = refs[parts : parts + 2]
    step = pl.program_id(1)

    @pl.when(step == 0)
    def _():
        total = jnp.zeros(scale.shape, f32)
        for block in blocks:
            values = block[...].astype(f32)
            total = total + jnp.sum(values * values, axis=-1, keepdims=True)
        scale[...] = lax.rsqrt(total / depth + epsilon)

    for at, block in enumerate(blocks):

        @pl.when(step == at)
        def _(block=block):
            out[...] = (block[...].astype(f32) * scale[...]).astype(out.dtype)


def normalize(own, parts, place):
    rows, width = own.shape
    depth = width * parts
    blocks = [own] + [lax.ppermute(own, "mp", around(parts, step)) for step in range(1, parts)]
    tile = min(256, rows)
    block = pl.BlockSpec((tile, width), lambda i, j, at: (i, 0))
    return pl.pallas_call(
        functools.partial(norm_kernel, parts, depth),
        grid_spec=pltpu.PrefetchScalarGridSpec(
            num_scalar_prefetch=1,
            grid=(rows // tile, parts),
            in_specs=[block] * parts,
            out_specs=[
                pl.BlockSpec(
                    (tile, width), lambda i, j, at: (i, lax.rem(at[0] + parts - j, parts))
                ),
                pl.BlockSpec((tile, 1), lambda i, j, at: (i, 0)),
            ],
        ),
        out_shape=[
            jax.ShapeDtypeStruct((rows, depth), bf16),
            jax.ShapeDtypeStruct((rows, 1), f32),
        ],
        compiler_params=params(),
        cost_estimate=cost(0, 4 * rows * depth),
    )(place.reshape(1).astype(jnp.int32), *blocks)


def grad_kernel(factor, normed, slope, out):
    product = lax.dot_general(normed[...], slope[...], OVER_ROWS, preferred_element_type=f32)
    out[...] = (product * factor).astype(out.dtype).reshape(out.shape)


def last_level_grad(normed, slope, factor, levels):
    rows, depth = normed.shape
    columns = slope.shape[1]
    tile = min(512, depth)
    return pl.pallas_call(
        functools.partial(grad_kernel, factor),
        grid=(depth // tile,),
        in_specs=[
            pl.BlockSpec((rows, tile), lambda i: (0, i)),
            pl.BlockSpec((rows, columns), lambda i: (0, 0)),
        ],
        out_specs=pl.BlockSpec((1, 1, tile, columns), lambda i: (0, levels - 1, i, 0)),
        out_shape=jax.ShapeDtypeStruct((1, levels, depth, columns), bf16),
        compiler_params=params(30),
        cost_estimate=cost(
            2 * rows * depth * columns, 2 * (rows * depth + rows * columns + depth * columns)
        ),
    )(normed, slope)


def state_kernel(factor, normed, weight, state, following, gate):
    pre = jnp.dot(normed[...], weight[...], preferred_element_type=f32) * factor
    sigmoid_part = jax.nn.sigmoid(pre)
    following[...] = (state[...].astype(f32) + pre * sigmoid_part).astype(bf16)
    gate[...] = sigmoid_part * (1.0 + pre * (1.0 - sigmoid_part))


def first_forward(normed, weight, state, factor):
    rows, depth = normed.shape
    columns = weight.shape[1]
    tile = min(256, rows)
    mine = pl.BlockSpec((tile, columns), lambda i: (i, 0))
    return pl.pallas_call(
        functools.partial(state_kernel, factor),
        grid=(rows // tile,),
        in_specs=[
            pl.BlockSpec((tile, depth), lambda i: (i, 0)),
            pl.BlockSpec((depth, columns), lambda i: (0, 0)),
            mine,
        ],
        out_specs=[mine, mine],
        out_shape=[
            jax.ShapeDtypeStruct((rows, columns), bf16),
            jax.ShapeDtypeStruct((rows, columns), f32),
        ],
        compiler_params=params(),
        cost_estimate=cost(
            2 * rows * depth * columns,
            2 * (rows * depth + 4 * rows * columns + depth * columns),
            rows * columns,
        ),
    )(normed, weight, state)


def slope_kernel(factor, width, at, normed, weight, upstream, slope, share, message):
    pre = jnp.dot(normed[...], weight[...], preferred_element_type=f32) * factor
    value = (upstream[...].astype(f32) * silu_slope(pre)).astype(bf16)
    slope[...] = value
    total = jnp.sum(value.astype(f32) * pre, axis=-1, keepdims=True)
    total = jnp.broadcast_to(total, (total.shape[0], 128)).T[: share.shape[0]]
    share[...] = total
    start = pl.multiple_of(at[0] * width, width)
    product = lax.dot_general(
        value, weight[pl.ds(start, width), :], OVER_COLUMNS, preferred_element_type=f32
    )
    height = value.shape[0]
    message[0, :height, :] = (product * factor).astype(message.dtype)
    high = total.astype(message.dtype)
    total = total - high.astype(f32)
    middle = total.astype(message.dtype)
    low = (total - middle.astype(f32)).astype(message.dtype)
    at = lax.broadcasted_iota(jnp.int32, total.shape, 0)
    pieces = jnp.where(at == 0, high.astype(f32), jnp.where(at == 1, middle.astype(f32), 0.0))
    pieces = jnp.where(at == 2, low.astype(f32), pieces)
    pieces = jnp.concatenate([pieces, jnp.zeros_like(pieces)], axis=0)
    message[0, height:, :] = pieces.astype(message.dtype)


def second_forward(normed, weight, upstream, where, width, factor):
    rows, depth = normed.shape
    columns = weight.shape[1]
    tile = width
    steps = rows // tile
    mine = pl.BlockSpec((tile, columns), lambda i, at: (i, 0))
    return pl.pallas_call(
        functools.partial(slope_kernel, factor, width),
        grid_spec=pltpu.PrefetchScalarGridSpec(
            num_scalar_prefetch=1,
            grid=(steps,),
            in_specs=[
                pl.BlockSpec((tile, depth), lambda i, at: (i, 0)),
                pl.BlockSpec((depth, columns), lambda i, at: (0, 0)),
                mine,
            ],
            out_specs=[
                mine,
                pl.BlockSpec((8, tile), lambda i, at: (0, i)),
                pl.BlockSpec((1, tile + 16, width), lambda i, at: (i, 0, 0)),
            ],
        ),
        out_shape=[
            jax.ShapeDtypeStruct((rows, columns), bf16),
            jax.ShapeDtypeStruct((8, rows), f32),
            jax.ShapeDtypeStruct((steps, tile + 16, width), bf16),
        ],
        compiler_params=params(),
        cost_estimate=cost(
            2 * rows * columns * (depth + width) // LIGHT,
            2 * (rows * (depth + 2 * columns) + depth * columns) // LIGHT,
        ),
    )(where.reshape(1).astype(jnp.int32), normed, weight, upstream)


def term_kernel(factor, where, slope, weight, out):
    product = lax.dot_general(slope[...], weight[...], OVER_COLUMNS, preferred_element_type=f32)
    out[...] = (product * factor).astype(out.dtype)


def term(slope, weight, where, width, factor):
    rows, columns = slope.shape
    tile = min(512, rows)
    return pl.pallas_call(
        functools.partial(term_kernel, factor),
        grid_spec=pltpu.PrefetchScalarGridSpec(
            num_scalar_prefetch=1,
            grid=(rows // tile,),
            in_specs=[
                pl.BlockSpec((tile, columns), lambda i, at: (i, 0)),
                pl.BlockSpec((width, columns), lambda i, at: (at[0], 0)),
            ],
            out_specs=pl.BlockSpec((tile, width), lambda i, at: (i, 0)),
        ),
        out_shape=jax.ShapeDtypeStruct((rows, width), bf16),
        compiler_params=params(30),
        cost_estimate=cost(
            2 * rows * columns * width // LIGHT,
            2 * (rows * columns + columns * width + rows * width) // LIGHT,
        ),
    )(where.reshape(1).astype(jnp.int32), slope, weight)


def first_kernel(factor, runs, *refs):
    normed, scale, share, upstream, state, gate, kept = refs[:7]
    terms = refs[7:-4]
    out, slope, total = refs[-3:]
    tile, columns = slope.shape
    width = columns // runs
    count = len(terms) // runs
    step = pl.program_id(0)
    last = pl.num_programs(0) - 1
    for run in range(runs):
        here = slice(run * width, (run + 1) * width)
        normed_grad = kept[:, here].astype(f32)
        for other in terms[run * count : (run + 1) * count]:
            arrived = other[0, :tile, :] if len(other.shape) == 3 else other[...]
            normed_grad = normed_grad + arrived.astype(f32)
        state_grad = (
            upstream[:, here].astype(f32)
            + scale[...] * normed_grad
            - state[:, here].astype(f32) * share[...]
        )
        slope[:, here] = (state_grad * gate[:, here]).astype(bf16)
    product = lax.dot_general(normed[...], slope[...], OVER_ROWS, preferred_element_type=f32)

    @pl.when(step == 0)
    def _():
        total[...] = product

    @pl.when(jnp.logical_and(step > 0, step < last))
    def _():
        total[...] = total[...] + product

    @pl.when(step == last)
    def _():
        whole = jnp.where(step > 0, total[...] + product, product)
        out[...] = (whole * factor).astype(out.dtype).reshape(out.shape)


def first_level_grad(normed, scale, share, mine, terms, runs, block, width, tile, factor, grads):
    rows, depth = normed.shape
    columns = runs * width
    column = pl.BlockSpec((tile, 1), lambda i: (i, 0))
    part = pl.BlockSpec((tile, columns), lambda i: (i, block))
    message = pl.BlockSpec((1, tile + 16, width), lambda i: (i, 0, 0))
    plain = pl.BlockSpec((tile, width), lambda i: (i, 0))
    return pl.pallas_call(
        functools.partial(first_kernel, factor, runs),
        grid=(rows // tile,),
        in_specs=[pl.BlockSpec((tile, depth), lambda i: (i, 0)), column, column]
        + [part] * len(mine)
        + [message if value.ndim == 3 else plain for value in terms]
        + [pl.BlockSpec(memory_space=pl.ANY)],
        out_specs=pl.BlockSpec((1, 1, depth, columns), lambda i: (0, 0, 0, block)),
        out_shape=jax.ShapeDtypeStruct(grads.shape, bf16),
        scratch_shapes=[pltpu.VMEM((tile, columns), bf16), pltpu.VMEM((depth, columns), f32)],
        input_output_aliases={3 + len(mine) + len(terms): 0},
        compiler_params=params(44),
        cost_estimate=cost(
            2 * rows * depth * columns * HEAVY,
            2 * (rows * depth + 7 * rows * columns + depth * columns) * HEAVY,
        ),
    )(normed, scale, share, *mine, *terms, grads)


def around(parts, step):
    return [(p, (p + step) % parts) for p in range(parts)]


def after(value, *others):
    return lax.optimization_barrier((value, *others))[0]


def shards(anchor, momentum, deltas, old_path, new_path, tokens, cotangent):
    groups = lax.axis_size("group")
    parts = lax.axis_size("mp")
    place = lax.axis_index("mp")
    levels = deltas.shape[1]
    depth = deltas.shape[2]
    columns = deltas.shape[3]
    factor = 1.0 / math.sqrt(depth)

    def exchange(blocks):
        return lax.all_to_all(blocks, "group", split_axis=0, concat_axis=0, tiled=True)

    received = [exchange(cast_level(deltas, level, groups)) for level in range(levels)]
    first_normed, _ = normalize(tokens[0], parts, place)
    received[0] = after(received[0], first_normed)

    previous = None
    loaded = []
    for level in range(levels):
        part_anchor, part_momentum, outgoing = outer_update(
            received[level],
            anchor,
            momentum,
            old_path[:, level],
            new_path[:, level],
            level,
            levels,
            previous,
        )
        previous = (part_anchor, part_momentum)
        loaded.append(exchange(outgoing).reshape(depth, columns))
    new_anchor, new_momentum = previous
    first_weight, second_weight = loaded

    upstream = cotangent[0]
    second_state, gate = first_forward(first_normed, first_weight, tokens[0], factor)
    second_normed, second_scale = normalize(second_state, parts, place)

    own_features = depth // parts
    width = min(RUN, own_features)
    runs = own_features // width

    def place_of(step, run):
        return lax.rem(place + step, parts) * runs + run

    def send(values):
        return [lax.ppermute(values[n], "mp", around(parts, n + 1)) for n in range(len(values))]

    def terms_of(source, run, steps):
        return [
            term(source, second_weight, place_of(step, run), width, factor) for step in steps
        ]

    rows = second_normed.shape[0]
    slope, own_share, message = second_forward(
        second_normed, second_weight, upstream, place_of(1, 0), width, factor
    )
    message = lax.ppermute(message, "mp", around(parts, 1))
    share = own_share[0] + jnp.sum(message[:, width : width + 3].astype(f32), axis=1).reshape(-1)
    arrived = [[message]]
    for step in range(2, parts):
        share = share + lax.ppermute(own_share, "mp", around(parts, step))[0]
        [value] = terms_of(slope, 0, [step])
        arrived[0].append(lax.ppermute(value, "mp", around(parts, step)))
    source = slope
    kept = grads = None
    for run in range(1, runs + 2):
        if run < runs:
            sent = terms_of(source, run, range(1, parts))
            arrived.append(send(sent))
            source = after(slope, sent[0])
        if kept is None:
            kept = term(source, second_weight, place, own_features, factor)
            source = after(slope, kept)
        elif grads is None:
            grads = last_level_grad(second_normed, source, factor, levels)
            source = after(slope, grads)
        if run < runs:
            source = after(source, *arrived[run - 1])
    scaled = second_scale**2 * after(share, grads).reshape(rows, 1) / depth
    mine = [upstream, second_state, gate, kept]
    bounds = [0, runs - 1, runs] if runs > 1 else [0, runs]
    for begin, end in zip(bounds[:-1], bounds[1:]):
        terms = [value for run in range(begin, end) for value in arrived[run]]
        grads = first_level_grad(
            first_normed,
            second_scale,
            scaled,
            mine,
            terms,
            end - begin,
            begin // (end - begin),
            width,
            width,
            factor,
            grads,
        )
    return (new_anchor, new_momentum, grads)


def solution(mesh):
    in_specs = (
        P(None, "group", "mp"),
        P(None, "group", "mp"),
        P("group", None, None, "mp"),
        P(),
        P(),
        P("group", None, "mp"),
        P("group", None, "mp"),
    )
    out_specs = (P(None, "group", "mp"), P(None, "group", "mp"), P("group", None, None, "mp"))
    return jax.shard_map(shards, mesh=mesh, in_specs=in_specs, out_specs=out_specs, check_vma=False)
```

```python
import functools
import math

import jax
import jax.numpy as jnp
from jax import lax
from jax.experimental import pallas as pl
from jax.experimental.pallas import tpu as pltpu
from jax.sharding import PartitionSpec as P

outer_rate = 0.7
momentum_rate = 0.9
epsilon = 1e-06

MEBI = 1024 * 1024
RUN = 256
LIGHT = 16
HEAVY = 4

f32 = jnp.float32
bf16 = jnp.bfloat16


def params(mebi=60):
    return pltpu.CompilerParams(vmem_limit_bytes=mebi * MEBI)


def silu_slope(values):
    sigmoid_part = jax.nn.sigmoid(values)
    return sigmoid_part * (1.0 + values * (1.0 - sigmoid_part))


def cast_kernel(src, dst):
    dst[...] = src[...].reshape(dst.shape).astype(dst.dtype)


def cast_level(deltas, level, groups):
    _, _, depth, columns = deltas.shape
    rows = depth // groups
    per = 8 if groups % 8 == 0 else 1
    return pl.pallas_call(
        cast_kernel,
        grid=(groups // per,),
        in_specs=[pl.BlockSpec((1, 1, per * rows, columns), lambda i: (0, level, i, 0))],
        out_specs=pl.BlockSpec((per, rows, columns), lambda i: (i, 0, 0)),
        out_shape=jax.ShapeDtypeStruct((groups, rows, columns), bf16),
        compiler_params=params(),
        cost_estimate=pl.CostEstimate(
            flops=0, bytes_accessed=depth * columns * 6, transcendentals=0
        ),
    )(deltas)


def update_kernel(groups, mods, aliased, old, new, received, anchor, momentum, *rest):
    new_anchor, new_momentum, outgoing, total = rest[2:] if aliased else rest
    total[...] = jnp.zeros_like(total)
    for g in range(groups):
        m = old[g]
        total[m] = total[m] + received[g].astype(f32)
    for m in range(mods):
        count = jnp.int32(0)
        for g in range(groups):
            count = count + jnp.where(old[g] == m, 1, 0)
        outer_grad = total[m] / count.astype(f32)
        moved = momentum_rate * momentum[m] + outer_grad
        new_momentum[m] = moved
        total[m] = anchor[m] - outer_rate * (outer_grad + momentum_rate * moved)
        new_anchor[m] = total[m]
    for g in range(groups):
        outgoing[g] = total[new[g]].astype(outgoing.dtype)


def outer_update(received, anchor, momentum, old, new, level, levels, previous):
    groups, rows, columns = received.shape
    modules = anchor.shape[0]
    mods = modules // levels
    tile = 32 if rows % 32 == 0 else rows
    state = pl.BlockSpec((mods, tile, columns), lambda i, *_: (level, i, 0))
    block = pl.BlockSpec((groups, tile, columns), lambda i, *_: (0, i, 0))
    anywhere = pl.BlockSpec(memory_space=pl.ANY)
    aliased = previous is not None
    whole = jax.ShapeDtypeStruct(anchor.shape, f32)
    return pl.pallas_call(
        functools.partial(update_kernel, groups, mods, aliased),
        grid_spec=pltpu.PrefetchScalarGridSpec(
            num_scalar_prefetch=2,
            grid=(rows // tile,),
            in_specs=[block, state, state] + ([anywhere, anywhere] if aliased else []),
            out_specs=[state, state, block],
            scratch_shapes=[pltpu.VMEM((mods, tile, columns), f32)],
        ),
        out_shape=[whole, whole, jax.ShapeDtypeStruct(received.shape, bf16)],
        input_output_aliases={5: 0, 6: 1} if aliased else {},
        compiler_params=params(),
        cost_estimate=pl.CostEstimate(
            flops=0,
            bytes_accessed=rows * columns * (groups * 4 + mods * 16),
            transcendentals=0,
        ),
    )(old, new, received, anchor, momentum, *(previous or ()))


OVER_ROWS = (((0,), (0,)), ((), ()))
OVER_COLUMNS = (((1,), (1,)), ((), ()))


def cost(flops, values, transcendentals=0):
    return pl.CostEstimate(flops=flops, bytes_accessed=values, transcendentals=transcendentals)


def norm_kernel(parts, depth, place, *refs):
    blocks = refs[:parts]
    out, scale = refs[parts : parts + 2]
    step = pl.program_id(1)

    @pl.when(step == 0)
    def _():
        total = jnp.zeros(scale.shape, f32)
        for block in blocks:
            values = block[...].astype(f32)
            total = total + jnp.sum(values * values, axis=-1, keepdims=True)
        scale[...] = lax.rsqrt(total / depth + epsilon)

    for at, block in enumerate(blocks):

        @pl.when(step == at)
        def _(block=block):
            out[...] = (block[...].astype(f32) * scale[...]).astype(out.dtype)


def normalize(own, parts, place):
    rows, width = own.shape
    depth = width * parts
    blocks = [own] + [lax.ppermute(own, "mp", around(parts, step)) for step in range(1, parts)]
    tile = min(256, rows)
    block = pl.BlockSpec((tile, width), lambda i, j, at: (i, 0))
    return pl.pallas_call(
        functools.partial(norm_kernel, parts, depth),
        grid_spec=pltpu.PrefetchScalarGridSpec(
            num_scalar_prefetch=1,
            grid=(rows // tile, parts),
            in_specs=[block] * parts,
            out_specs=[
                pl.BlockSpec(
                    (tile, width), lambda i, j, at: (i, lax.rem(at[0] + parts - j, parts))
                ),
                pl.BlockSpec((tile, 1), lambda i, j, at: (i, 0)),
            ],
        ),
        out_shape=[
            jax.ShapeDtypeStruct((rows, depth), bf16),
            jax.ShapeDtypeStruct((rows, 1), f32),
        ],
        compiler_params=params(),
        cost_estimate=cost(0, 4 * rows * depth),
    )(place.reshape(1).astype(jnp.int32), *blocks)


def grad_kernel(factor, normed, slope, out):
    product = lax.dot_general(normed[...], slope[...], OVER_ROWS, preferred_element_type=f32)
    out[...] = (product * factor).astype(out.dtype).reshape(out.shape)


def last_level_grad(normed, slope, factor, levels):
    rows, depth = normed.shape
    columns = slope.shape[1]
    tile = min(512, depth)
    return pl.pallas_call(
        functools.partial(grad_kernel, factor),
        grid=(depth // tile,),
        in_specs=[
            pl.BlockSpec((rows, tile), lambda i: (0, i)),
            pl.BlockSpec((rows, columns), lambda i: (0, 0)),
        ],
        out_specs=pl.BlockSpec((1, 1, tile, columns), lambda i: (0, levels - 1, i, 0)),
        out_shape=jax.ShapeDtypeStruct((1, levels, depth, columns), bf16),
        compiler_params=params(30),
        cost_estimate=cost(
            2 * rows * depth * columns, 2 * (rows * depth + rows * columns + depth * columns)
        ),
    )(normed, slope)


def state_kernel(factor, normed, weight, state, following, gate):
    pre = jnp.dot(normed[...], weight[...], preferred_element_type=f32) * factor
    sigmoid_part = jax.nn.sigmoid(pre)
    following[...] = (state[...].astype(f32) + pre * sigmoid_part).astype(bf16)
    gate[...] = sigmoid_part * (1.0 + pre * (1.0 - sigmoid_part))


def first_forward(normed, weight, state, factor):
    rows, depth = normed.shape
    columns = weight.shape[1]
    tile = min(256, rows)
    mine = pl.BlockSpec((tile, columns), lambda i: (i, 0))
    return pl.pallas_call(
        functools.partial(state_kernel, factor),
        grid=(rows // tile,),
        in_specs=[
            pl.BlockSpec((tile, depth), lambda i: (i, 0)),
            pl.BlockSpec((depth, columns), lambda i: (0, 0)),
            mine,
        ],
        out_specs=[mine, mine],
        out_shape=[
            jax.ShapeDtypeStruct((rows, columns), bf16),
            jax.ShapeDtypeStruct((rows, columns), f32),
        ],
        compiler_params=params(),
        cost_estimate=cost(
            2 * rows * depth * columns,
            2 * (rows * depth + 4 * rows * columns + depth * columns),
            rows * columns,
        ),
    )(normed, weight, state)


def slope_kernel(factor, width, at, normed, weight, upstream, slope, share, message):
    pre = jnp.dot(normed[...], weight[...], preferred_element_type=f32) * factor
    value = (upstream[...].astype(f32) * silu_slope(pre)).astype(bf16)
    slope[...] = value
    total = jnp.sum(value.astype(f32) * pre, axis=-1, keepdims=True)
    total = jnp.broadcast_to(total, (total.shape[0], 128)).T[: share.shape[0]]
    share[...] = total
    start = pl.multiple_of(at[0] * width, width)
    product = lax.dot_general(
        value, weight[pl.ds(start, width), :], OVER_COLUMNS, preferred_element_type=f32
    )
    height = value.shape[0]
    message[0, :height, :] = (product * factor).astype(message.dtype)
    high = total.astype(message.dtype)
    total = total - high.astype(f32)
    middle = total.astype(message.dtype)
    low = (total - middle.astype(f32)).astype(message.dtype)
    at = lax.broadcasted_iota(jnp.int32, total.shape, 0)
    pieces = jnp.where(at == 0, high.astype(f32), jnp.where(at == 1, middle.astype(f32), 0.0))
    pieces = jnp.where(at == 2, low.astype(f32), pieces)
    pieces = jnp.concatenate([pieces, jnp.zeros_like(pieces)], axis=0)
    message[0, height:, :] = pieces.astype(message.dtype)


def second_forward(normed, weight, upstream, where, width, factor):
    rows, depth = normed.shape
    columns = weight.shape[1]
    tile = width
    steps = rows // tile
    mine = pl.BlockSpec((tile, columns), lambda i, at: (i, 0))
    return pl.pallas_call(
        functools.partial(slope_kernel, factor, width),
        grid_spec=pltpu.PrefetchScalarGridSpec(
            num_scalar_prefetch=1,
            grid=(steps,),
            in_specs=[
                pl.BlockSpec((tile, depth), lambda i, at: (i, 0)),
                pl.BlockSpec((depth, columns), lambda i, at: (0, 0)),
                mine,
            ],
            out_specs=[
                mine,
                pl.BlockSpec((8, tile), lambda i, at: (0, i)),
                pl.BlockSpec((1, tile + 16, width), lambda i, at: (i, 0, 0)),
            ],
        ),
        out_shape=[
            jax.ShapeDtypeStruct((rows, columns), bf16),
            jax.ShapeDtypeStruct((8, rows), f32),
            jax.ShapeDtypeStruct((steps, tile + 16, width), bf16),
        ],
        compiler_params=params(),
        cost_estimate=cost(
            2 * rows * columns * (depth + width) // LIGHT,
            2 * (rows * (depth + 2 * columns) + depth * columns) // LIGHT,
        ),
    )(where.reshape(1).astype(jnp.int32), normed, weight, upstream)


def term_kernel(factor, where, slope, weight, out):
    product = lax.dot_general(slope[...], weight[...], OVER_COLUMNS, preferred_element_type=f32)
    out[...] = (product * factor).astype(out.dtype)


def term(slope, weight, where, width, factor):
    rows, columns = slope.shape
    tile = min(512, rows)
    return pl.pallas_call(
        functools.partial(term_kernel, factor),
        grid_spec=pltpu.PrefetchScalarGridSpec(
            num_scalar_prefetch=1,
            grid=(rows // tile,),
            in_specs=[
                pl.BlockSpec((tile, columns), lambda i, at: (i, 0)),
                pl.BlockSpec((width, columns), lambda i, at: (at[0], 0)),
            ],
            out_specs=pl.BlockSpec((tile, width), lambda i, at: (i, 0)),
        ),
        out_shape=jax.ShapeDtypeStruct((rows, width), bf16),
        compiler_params=params(30),
        cost_estimate=cost(
            2 * rows * columns * width // LIGHT,
            2 * (rows * columns + columns * width + rows * width) // LIGHT,
        ),
    )(where.reshape(1).astype(jnp.int32), slope, weight)


def first_kernel(factor, runs, *refs):
    normed, scale, share, upstream, state, gate, kept = refs[:7]
    terms = refs[7:-4]
    out, slope, total = refs[-3:]
    tile, columns = slope.shape
    width = columns // runs
    count = len(terms) // runs
    step = pl.program_id(0)
    last = pl.num_programs(0) - 1
    for run in range(runs):
        here = slice(run * width, (run + 1) * width)
        normed_grad = kept[:, here].astype(f32)
        for other in terms[run * count : (run + 1) * count]:
            arrived = other[0, :tile, :] if len(other.shape) == 3 else other[...]
            normed_grad = normed_grad + arrived.astype(f32)
        state_grad = (
            upstream[:, here].astype(f32)
            + scale[...] * normed_grad
            - state[:, here].astype(f32) * share[...]
        )
        slope[:, here] = (state_grad * gate[:, here]).astype(bf16)
    product = lax.dot_general(normed[...], slope[...], OVER_ROWS, preferred_element_type=f32)

    @pl.when(step == 0)
    def _():
        total[...] = product

    @pl.when(jnp.logical_and(step > 0, step < last))
    def _():
        total[...] = total[...] + product

    @pl.when(step == last)
    def _():
        whole = jnp.where(step > 0, total[...] + product, product)
        out[...] = (whole * factor).astype(out.dtype).reshape(out.shape)


def first_level_grad(normed, scale, share, mine, terms, runs, block, width, tile, factor, grads):
    rows, depth = normed.shape
    columns = runs * width
    column = pl.BlockSpec((tile, 1), lambda i: (i, 0))
    part = pl.BlockSpec((tile, columns), lambda i: (i, block))
    message = pl.BlockSpec((1, tile + 16, width), lambda i: (i, 0, 0))
    plain = pl.BlockSpec((tile, width), lambda i: (i, 0))
    return pl.pallas_call(
        functools.partial(first_kernel, factor, runs),
        grid=(rows // tile,),
        in_specs=[pl.BlockSpec((tile, depth), lambda i: (i, 0)), column, column]
        + [part] * len(mine)
        + [message if value.ndim == 3 else plain for value in terms]
        + [pl.BlockSpec(memory_space=pl.ANY)],
        out_specs=pl.BlockSpec((1, 1, depth, columns), lambda i: (0, 0, 0, block)),
        out_shape=jax.ShapeDtypeStruct(grads.shape, bf16),
        scratch_shapes=[pltpu.VMEM((tile, columns), bf16), pltpu.VMEM((depth, columns), f32)],
        input_output_aliases={3 + len(mine) + len(terms): 0},
        compiler_params=params(44),
        cost_estimate=cost(
            2 * rows * depth * columns * HEAVY,
            2 * (rows * depth + 7 * rows * columns + depth * columns) * HEAVY,
        ),
    )(normed, scale, share, *mine, *terms, grads)


def around(parts, step):
    return [(p, (p + step) % parts) for p in range(parts)]


def after(value, *others):
    return lax.optimization_barrier((value, *others))[0]


def shards(anchor, momentum, deltas, old_path, new_path, tokens, cotangent):
    groups = lax.axis_size("group")
    parts = lax.axis_size("mp")
    place = lax.axis_index("mp")
    levels = deltas.shape[1]
    depth = deltas.shape[2]
    columns = deltas.shape[3]
    factor = 1.0 / math.sqrt(depth)

    def exchange(blocks):
        return lax.all_to_all(blocks, "group", split_axis=0, concat_axis=0, tiled=True)

    received = [exchange(cast_level(deltas, level, groups)) for level in range(levels)]
    first_normed, _ = normalize(tokens[0], parts, place)
    received[0] = after(received[0], first_normed)

    previous = None
    loaded = []
    for level in range(levels):
        part_anchor, part_momentum, outgoing = outer_update(
            received[level],
            anchor,
            momentum,
            old_path[:, level],
            new_path[:, level],
            level,
            levels,
            previous,
        )
        previous = (part_anchor, part_momentum)
        loaded.append(exchange(outgoing).reshape(depth, columns))
    new_anchor, new_momentum = previous
    first_weight, second_weight = loaded

    upstream = cotangent[0]
    second_state, gate = first_forward(first_normed, first_weight, tokens[0], factor)
    second_normed, second_scale = normalize(second_state, parts, place)

    own_features = depth // parts
    width = min(RUN, own_features)
    runs = own_features // width

    def place_of(step, run):
        return lax.rem(place + step, parts) * runs + run

    def send(values):
        return [lax.ppermute(values[n], "mp", around(parts, n + 1)) for n in range(len(values))]

    def terms_of(source, run, steps):
        return [
            term(source, second_weight, place_of(step, run), width, factor) for step in steps
        ]

    rows = second_normed.shape[0]
    slope, own_share, message = second_forward(
        second_normed, second_weight, upstream, place_of(1, 0), width, factor
    )
    message = lax.ppermute(message, "mp", around(parts, 1))
    share = own_share[0] + jnp.sum(message[:, width : width + 3].astype(f32), axis=1).reshape(-1)
    arrived = [[message]]
    for step in range(2, parts):
        share = share + lax.ppermute(own_share, "mp", around(parts, step))[0]
        [value] = terms_of(slope, 0, [step])
        arrived[0].append(lax.ppermute(value, "mp", around(parts, step)))
    source = slope
    kept = grads = None
    for run in range(1, runs + 2):
        if run < runs:
            sent = terms_of(source, run, range(1, parts))
            arrived.append(send(sent))
            source = after(slope, sent[0])
        if kept is None:
            kept = term(source, second_weight, place, own_features, factor)
            source = after(slope, kept)
        elif grads is None:
            grads = last_level_grad(second_normed, source, factor, levels)
            source = after(slope, grads)
        if run < runs:
            source = after(source, *arrived[run - 1])
    scaled = second_scale**2 * after(share, grads).reshape(rows, 1) / depth
    mine = [upstream, second_state, gate, kept]
    bounds = [0, runs - 1, runs] if runs > 1 else [0, runs]
    for begin, end in zip(bounds[:-1], bounds[1:]):
        terms = [value for run in range(begin, end) for value in arrived[run]]
        grads = first_level_grad(
            first_normed,
            second_scale,
            scaled,
            mine,
            terms,
            end - begin,
            begin // (end - begin),
            width,
            width,
            factor,
            grads,
        )
    return (new_anchor, new_momentum, grads)


def solution(mesh):
    in_specs = (
        P(None, "group", "mp"),
        P(None, "group", "mp"),
        P("group", None, None, "mp"),
        P(),
        P(),
        P("group", None, "mp"),
        P("group", None, "mp"),
    )
    out_specs = (P(None, "group", "mp"), P(None, "group", "mp"), P("group", None, None, "mp"))
    return jax.shard_map(shards, mesh=mesh, in_specs=in_specs, out_specs=out_specs, check_vma=False)
```

```python
import functools
import math

import jax
import jax.numpy as jnp
from jax import lax
from jax.experimental import pallas as pl
from jax.experimental.pallas import tpu as pltpu
from jax.sharding import PartitionSpec as P

outer_rate = 0.7
momentum_rate = 0.9
epsilon = 1e-06

MEBI = 1024 * 1024
RUN = 256
LIGHT = 16
HEAVY = 4

f32 = jnp.float32
bf16 = jnp.bfloat16


def params(mebi=60):
    return pltpu.CompilerParams(vmem_limit_bytes=mebi * MEBI)


def silu_slope(values):
    sigmoid_part = jax.nn.sigmoid(values)
    return sigmoid_part * (1.0 + values * (1.0 - sigmoid_part))


def cast_kernel(src, dst):
    dst[...] = src[...].reshape(dst.shape).astype(dst.dtype)


def cast_level(deltas, level, groups):
    _, _, depth, columns = deltas.shape
    rows = depth // groups
    per = 8 if groups % 8 == 0 else 1
    return pl.pallas_call(
        cast_kernel,
        grid=(groups // per,),
        in_specs=[pl.BlockSpec((1, 1, per * rows, columns), lambda i: (0, level, i, 0))],
        out_specs=pl.BlockSpec((per, rows, columns), lambda i: (i, 0, 0)),
        out_shape=jax.ShapeDtypeStruct((groups, rows, columns), bf16),
        compiler_params=params(),
        cost_estimate=pl.CostEstimate(
            flops=0, bytes_accessed=depth * columns * 6, transcendentals=0
        ),
    )(deltas)


def update_kernel(groups, mods, aliased, old, new, received, anchor, momentum, *rest):
    new_anchor, new_momentum, outgoing, total = rest[2:] if aliased else rest
    total[...] = jnp.zeros_like(total)
    for g in range(groups):
        m = old[g]
        total[m] = total[m] + received[g].astype(f32)
    for m in range(mods):
        count = jnp.int32(0)
        for g in range(groups):
            count = count + jnp.where(old[g] == m, 1, 0)
        outer_grad = total[m] / count.astype(f32)
        moved = momentum_rate * momentum[m] + outer_grad
        new_momentum[m] = moved
        total[m] = anchor[m] - outer_rate * (outer_grad + momentum_rate * moved)
        new_anchor[m] = total[m]
    for g in range(groups):
        outgoing[g] = total[new[g]].astype(outgoing.dtype)


def outer_update(received, anchor, momentum, old, new, level, levels, previous):
    groups, rows, columns = received.shape
    modules = anchor.shape[0]
    mods = modules // levels
    tile = 32 if rows % 32 == 0 else rows
    state = pl.BlockSpec((mods, tile, columns), lambda i, *_: (level, i, 0))
    block = pl.BlockSpec((groups, tile, columns), lambda i, *_: (0, i, 0))
    anywhere = pl.BlockSpec(memory_space=pl.ANY)
    aliased = previous is not None
    whole = jax.ShapeDtypeStruct(anchor.shape, f32)
    return pl.pallas_call(
        functools.partial(update_kernel, groups, mods, aliased),
        grid_spec=pltpu.PrefetchScalarGridSpec(
            num_scalar_prefetch=2,
            grid=(rows // tile,),
            in_specs=[block, state, state] + ([anywhere, anywhere] if aliased else []),
            out_specs=[state, state, block],
            scratch_shapes=[pltpu.VMEM((mods, tile, columns), f32)],
        ),
        out_shape=[whole, whole, jax.ShapeDtypeStruct(received.shape, bf16)],
        input_output_aliases={5: 0, 6: 1} if aliased else {},
        compiler_params=params(),
        cost_estimate=pl.CostEstimate(
            flops=0,
            bytes_accessed=rows * columns * (groups * 4 + mods * 16),
            transcendentals=0,
        ),
    )(old, new, received, anchor, momentum, *(previous or ()))


OVER_ROWS = (((0,), (0,)), ((), ()))
OVER_COLUMNS = (((1,), (1,)), ((), ()))


def cost(flops, values, transcendentals=0):
    return pl.CostEstimate(flops=flops, bytes_accessed=values, transcendentals=transcendentals)


def norm_kernel(parts, depth, place, *refs):
    blocks = refs[:parts]
    out, scale = refs[parts : parts + 2]
    step = pl.program_id(1)

    @pl.when(step == 0)
    def _():
        total = jnp.zeros(scale.shape, f32)
        for block in blocks:
            values = block[...].astype(f32)
            total = total + jnp.sum(values * values, axis=-1, keepdims=True)
        scale[...] = lax.rsqrt(total / depth + epsilon)

    for at, block in enumerate(blocks):

        @pl.when(step == at)
        def _(block=block):
            out[...] = (block[...].astype(f32) * scale[...]).astype(out.dtype)


def normalize(own, parts, place):
    rows, width = own.shape
    depth = width * parts
    blocks = [own] + [lax.ppermute(own, "mp", around(parts, step)) for step in range(1, parts)]
    tile = min(256, rows)
    block = pl.BlockSpec((tile, width), lambda i, j, at: (i, 0))
    return pl.pallas_call(
        functools.partial(norm_kernel, parts, depth),
        grid_spec=pltpu.PrefetchScalarGridSpec(
            num_scalar_prefetch=1,
            grid=(rows // tile, parts),
            in_specs=[block] * parts,
            out_specs=[
                pl.BlockSpec(
                    (tile, width), lambda i, j, at: (i, lax.rem(at[0] + parts - j, parts))
                ),
                pl.BlockSpec((tile, 1), lambda i, j, at: (i, 0)),
            ],
        ),
        out_shape=[
            jax.ShapeDtypeStruct((rows, depth), bf16),
            jax.ShapeDtypeStruct((rows, 1), f32),
        ],
        compiler_params=params(),
        cost_estimate=cost(0, 4 * rows * depth),
    )(place.reshape(1).astype(jnp.int32), *blocks)


def grad_kernel(factor, normed, slope, out):
    product = lax.dot_general(normed[...], slope[...], OVER_ROWS, preferred_element_type=f32)
    out[...] = (product * factor).astype(out.dtype).reshape(out.shape)


def last_level_grad(normed, slope, factor, levels):
    rows, depth = normed.shape
    columns = slope.shape[1]
    tile = min(512, depth)
    return pl.pallas_call(
        functools.partial(grad_kernel, factor),
        grid=(depth // tile,),
        in_specs=[
            pl.BlockSpec((rows, tile), lambda i: (0, i)),
            pl.BlockSpec((rows, columns), lambda i: (0, 0)),
        ],
        out_specs=pl.BlockSpec((1, 1, tile, columns), lambda i: (0, levels - 1, i, 0)),
        out_shape=jax.ShapeDtypeStruct((1, levels, depth, columns), bf16),
        compiler_params=params(30),
        cost_estimate=cost(
            2 * rows * depth * columns, 2 * (rows * depth + rows * columns + depth * columns)
        ),
    )(normed, slope)


def state_kernel(factor, normed, weight, state, following, gate):
    pre = jnp.dot(normed[...], weight[...], preferred_element_type=f32) * factor
    sigmoid_part = jax.nn.sigmoid(pre)
    following[...] = (state[...].astype(f32) + pre * sigmoid_part).astype(bf16)
    gate[...] = sigmoid_part * (1.0 + pre * (1.0 - sigmoid_part))


def first_forward(normed, weight, state, factor):
    rows, depth = normed.shape
    columns = weight.shape[1]
    tile = min(256, rows)
    mine = pl.BlockSpec((tile, columns), lambda i: (i, 0))
    return pl.pallas_call(
        functools.partial(state_kernel, factor),
        grid=(rows // tile,),
        in_specs=[
            pl.BlockSpec((tile, depth), lambda i: (i, 0)),
            pl.BlockSpec((depth, columns), lambda i: (0, 0)),
            mine,
        ],
        out_specs=[mine, mine],
        out_shape=[
            jax.ShapeDtypeStruct((rows, columns), bf16),
            jax.ShapeDtypeStruct((rows, columns), f32),
        ],
        compiler_params=params(),
        cost_estimate=cost(
            2 * rows * depth * columns,
            2 * (rows * depth + 4 * rows * columns + depth * columns),
            rows * columns,
        ),
    )(normed, weight, state)


def slope_kernel(factor, width, at, normed, weight, upstream, slope, share, message):
    pre = jnp.dot(normed[...], weight[...], preferred_element_type=f32) * factor
    value = (upstream[...].astype(f32) * silu_slope(pre)).astype(bf16)
    slope[...] = value
    total = jnp.sum(value.astype(f32) * pre, axis=-1, keepdims=True)
    total = jnp.broadcast_to(total, (total.shape[0], 128)).T[: share.shape[0]]
    share[...] = total
    start = pl.multiple_of(at[0] * width, width)
    product = lax.dot_general(
        value, weight[pl.ds(start, width), :], OVER_COLUMNS, preferred_element_type=f32
    )
    height = value.shape[0]
    message[0, :height, :] = (product * factor).astype(message.dtype)
    high = total.astype(message.dtype)
    total = total - high.astype(f32)
    middle = total.astype(message.dtype)
    low = (total - middle.astype(f32)).astype(message.dtype)
    at = lax.broadcasted_iota(jnp.int32, total.shape, 0)
    pieces = jnp.where(at == 0, high.astype(f32), jnp.where(at == 1, middle.astype(f32), 0.0))
    pieces = jnp.where(at == 2, low.astype(f32), pieces)
    pieces = jnp.concatenate([pieces, jnp.zeros_like(pieces)], axis=0)
    message[0, height:, :] = pieces.astype(message.dtype)


def second_forward(normed, weight, upstream, where, width, factor):
    rows, depth = normed.shape
    columns = weight.shape[1]
    tile = width
    steps = rows // tile
    mine = pl.BlockSpec((tile, columns), lambda i, at: (i, 0))
    return pl.pallas_call(
        functools.partial(slope_kernel, factor, width),
        grid_spec=pltpu.PrefetchScalarGridSpec(
            num_scalar_prefetch=1,
            grid=(steps,),
            in_specs=[
                pl.BlockSpec((tile, depth), lambda i, at: (i, 0)),
                pl.BlockSpec((depth, columns), lambda i, at: (0, 0)),
                mine,
            ],
            out_specs=[
                mine,
                pl.BlockSpec((8, tile), lambda i, at: (0, i)),
                pl.BlockSpec((1, tile + 16, width), lambda i, at: (i, 0, 0)),
            ],
        ),
        out_shape=[
            jax.ShapeDtypeStruct((rows, columns), bf16),
            jax.ShapeDtypeStruct((8, rows), f32),
            jax.ShapeDtypeStruct((steps, tile + 16, width), bf16),
        ],
        compiler_params=params(),
        cost_estimate=cost(
            2 * rows * columns * (depth + width) // LIGHT,
            2 * (rows * (depth + 2 * columns) + depth * columns) // LIGHT,
        ),
    )(where.reshape(1).astype(jnp.int32), normed, weight, upstream)


def term_kernel(factor, where, slope, weight, out):
    product = lax.dot_general(slope[...], weight[...], OVER_COLUMNS, preferred_element_type=f32)
    out[...] = (product * factor).astype(out.dtype)


def term(slope, weight, where, width, factor):
    rows, columns = slope.shape
    tile = min(512, rows)
    return pl.pallas_call(
        functools.partial(term_kernel, factor),
        grid_spec=pltpu.PrefetchScalarGridSpec(
            num_scalar_prefetch=1,
            grid=(rows // tile,),
            in_specs=[
                pl.BlockSpec((tile, columns), lambda i, at: (i, 0)),
                pl.BlockSpec((width, columns), lambda i, at: (at[0], 0)),
            ],
            out_specs=pl.BlockSpec((tile, width), lambda i, at: (i, 0)),
        ),
        out_shape=jax.ShapeDtypeStruct((rows, width), bf16),
        compiler_params=params(30),
        cost_estimate=cost(
            2 * rows * columns * width // LIGHT,
            2 * (rows * columns + columns * width + rows * width) // LIGHT,
        ),
    )(where.reshape(1).astype(jnp.int32), slope, weight)


def first_kernel(factor, runs, *refs):
    normed, scale, share, upstream, state, gate, kept = refs[:7]
    terms = refs[7:-4]
    out, slope, total = refs[-3:]
    tile, columns = slope.shape
    width = columns // runs
    count = len(terms) // runs
    step = pl.program_id(0)
    last = pl.num_programs(0) - 1
    for run in range(runs):
        here = slice(run * width, (run + 1) * width)
        normed_grad = kept[:, here].astype(f32)
        for other in terms[run * count : (run + 1) * count]:
            arrived = other[0, :tile, :] if len(other.shape) == 3 else other[...]
            normed_grad = normed_grad + arrived.astype(f32)
        state_grad = (
            upstream[:, here].astype(f32)
            + scale[...] * normed_grad
            - state[:, here].astype(f32) * share[...]
        )
        slope[:, here] = (state_grad * gate[:, here]).astype(bf16)
    product = lax.dot_general(normed[...], slope[...], OVER_ROWS, preferred_element_type=f32)

    @pl.when(step == 0)
    def _():
        total[...] = product

    @pl.when(jnp.logical_and(step > 0, step < last))
    def _():
        total[...] = total[...] + product

    @pl.when(step == last)
    def _():
        whole = jnp.where(step > 0, total[...] + product, product)
        out[...] = (whole * factor).astype(out.dtype).reshape(out.shape)


def first_level_grad(normed, scale, share, mine, terms, runs, block, width, tile, factor, grads):
    rows, depth = normed.shape
    columns = runs * width
    column = pl.BlockSpec((tile, 1), lambda i: (i, 0))
    part = pl.BlockSpec((tile, columns), lambda i: (i, block))
    message = pl.BlockSpec((1, tile + 16, width), lambda i: (i, 0, 0))
    plain = pl.BlockSpec((tile, width), lambda i: (i, 0))
    return pl.pallas_call(
        functools.partial(first_kernel, factor, runs),
        grid=(rows // tile,),
        in_specs=[pl.BlockSpec((tile, depth), lambda i: (i, 0)), column, column]
        + [part] * len(mine)
        + [message if value.ndim == 3 else plain for value in terms]
        + [pl.BlockSpec(memory_space=pl.ANY)],
        out_specs=pl.BlockSpec((1, 1, depth, columns), lambda i: (0, 0, 0, block)),
        out_shape=jax.ShapeDtypeStruct(grads.shape, bf16),
        scratch_shapes=[pltpu.VMEM((tile, columns), bf16), pltpu.VMEM((depth, columns), f32)],
        input_output_aliases={3 + len(mine) + len(terms): 0},
        compiler_params=params(44),
        cost_estimate=cost(
            2 * rows * depth * columns * HEAVY,
            2 * (rows * depth + 7 * rows * columns + depth * columns) * HEAVY,
        ),
    )(normed, scale, share, *mine, *terms, grads)


def around(parts, step):
    return [(p, (p + step) % parts) for p in range(parts)]


def after(value, *others):
    return lax.optimization_barrier((value, *others))[0]


def shards(anchor, momentum, deltas, old_path, new_path, tokens, cotangent):
    groups = lax.axis_size("group")
    parts = lax.axis_size("mp")
    place = lax.axis_index("mp")
    levels = deltas.shape[1]
    depth = deltas.shape[2]
    columns = deltas.shape[3]
    factor = 1.0 / math.sqrt(depth)

    def exchange(blocks):
        return lax.all_to_all(blocks, "group", split_axis=0, concat_axis=0, tiled=True)

    received = [exchange(cast_level(deltas, level, groups)) for level in range(levels)]
    first_normed, _ = normalize(tokens[0], parts, place)
    received[0] = after(received[0], first_normed)

    previous = None
    loaded = []
    for level in range(levels):
        part_anchor, part_momentum, outgoing = outer_update(
            received[level],
            anchor,
            momentum,
            old_path[:, level],
            new_path[:, level],
            level,
            levels,
            previous,
        )
        previous = (part_anchor, part_momentum)
        loaded.append(exchange(outgoing).reshape(depth, columns))
    new_anchor, new_momentum = previous
    first_weight, second_weight = loaded

    upstream = cotangent[0]
    second_state, gate = first_forward(first_normed, first_weight, tokens[0], factor)
    second_normed, second_scale = normalize(second_state, parts, place)

    own_features = depth // parts
    width = min(RUN, own_features)
    runs = own_features // width

    def place_of(step, run):
        return lax.rem(place + step, parts) * runs + run

    def send(values):
        return [lax.ppermute(values[n], "mp", around(parts, n + 1)) for n in range(len(values))]

    def terms_of(source, run, steps):
        return [
            term(source, second_weight, place_of(step, run), width, factor) for step in steps
        ]

    rows = second_normed.shape[0]
    slope, own_share, message = second_forward(
        second_normed, second_weight, upstream, place_of(1, 0), width, factor
    )
    message = lax.ppermute(message, "mp", around(parts, 1))
    share = own_share[0] + jnp.sum(message[:, width : width + 3].astype(f32), axis=1).reshape(-1)
    arrived = [[message]]
    for step in range(2, parts):
        share = share + lax.ppermute(own_share, "mp", around(parts, step))[0]
        [value] = terms_of(slope, 0, [step])
        arrived[0].append(lax.ppermute(value, "mp", around(parts, step)))
    source = slope
    kept = grads = None
    for run in range(1, runs + 2):
        if run < runs:
            sent = terms_of(source, run, range(1, parts))
            arrived.append(send(sent))
            source = after(slope, sent[0])
        if kept is None:
            kept = term(source, second_weight, place, own_features, factor)
            source = after(slope, kept)
        elif grads is None:
            grads = last_level_grad(second_normed, source, factor, levels)
            source = after(slope, grads)
        if run < runs:
            source = after(source, *arrived[run - 1])
    scaled = second_scale**2 * after(share, grads).reshape(rows, 1) / depth
    mine = [upstream, second_state, gate, kept]
    bounds = [0] + list(range(max(1, runs - 2), runs + 1))
    for begin, end in zip(bounds[:-1], bounds[1:]):
        terms = [value for run in range(begin, end) for value in arrived[run]]
        grads = first_level_grad(
            first_normed,
            second_scale,
            scaled,
            mine,
            terms,
            end - begin,
            begin // (end - begin),
            width,
            width,
            factor,
            grads,
        )
    return (new_anchor, new_momentum, grads)


def solution(mesh):
    in_specs = (
        P(None, "group", "mp"),
        P(None, "group", "mp"),
        P("group", None, None, "mp"),
        P(),
        P(),
        P("group", None, "mp"),
        P("group", None, "mp"),
    )
    out_specs = (P(None, "group", "mp"), P(None, "group", "mp"), P("group", None, None, "mp"))
    return jax.shard_map(shards, mesh=mesh, in_specs=in_specs, out_specs=out_specs, check_vma=False)
```

```python
import functools
import math

import jax
import jax.numpy as jnp
from jax import lax
from jax.experimental import pallas as pl
from jax.experimental.pallas import tpu as pltpu
from jax.sharding import PartitionSpec as P

outer_rate = 0.7
momentum_rate = 0.9
epsilon = 1e-06

MEBI = 1024 * 1024
RUN = 256
LIGHT = 16
HEAVY = 4

f32 = jnp.float32
bf16 = jnp.bfloat16


def params(mebi=60):
    return pltpu.CompilerParams(vmem_limit_bytes=mebi * MEBI)


def silu_slope(values):
    sigmoid_part = jax.nn.sigmoid(values)
    return sigmoid_part * (1.0 + values * (1.0 - sigmoid_part))


def cast_kernel(src, dst):
    dst[...] = src[...].reshape(dst.shape).astype(dst.dtype)


def cast_level(deltas, level, groups):
    _, _, depth, columns = deltas.shape
    rows = depth // groups
    per = 8 if groups % 8 == 0 else 1
    return pl.pallas_call(
        cast_kernel,
        grid=(groups // per,),
        in_specs=[pl.BlockSpec((1, 1, per * rows, columns), lambda i: (0, level, i, 0))],
        out_specs=pl.BlockSpec((per, rows, columns), lambda i: (i, 0, 0)),
        out_shape=jax.ShapeDtypeStruct((groups, rows, columns), bf16),
        compiler_params=params(),
        cost_estimate=pl.CostEstimate(
            flops=0, bytes_accessed=depth * columns * 6, transcendentals=0
        ),
    )(deltas)


def update_kernel(groups, mods, aliased, old, new, received, anchor, momentum, *rest):
    new_anchor, new_momentum, outgoing, total = rest[2:] if aliased else rest
    total[...] = jnp.zeros_like(total)
    for g in range(groups):
        m = old[g]
        total[m] = total[m] + received[g].astype(f32)
    for m in range(mods):
        count = jnp.int32(0)
        for g in range(groups):
            count = count + jnp.where(old[g] == m, 1, 0)
        outer_grad = total[m] / count.astype(f32)
        moved = momentum_rate * momentum[m] + outer_grad
        new_momentum[m] = moved
        total[m] = anchor[m] - outer_rate * (outer_grad + momentum_rate * moved)
        new_anchor[m] = total[m]
    for g in range(groups):
        outgoing[g] = total[new[g]].astype(outgoing.dtype)


def outer_update(received, anchor, momentum, old, new, level, levels, previous):
    groups, rows, columns = received.shape
    modules = anchor.shape[0]
    mods = modules // levels
    tile = 32 if rows % 32 == 0 else rows
    state = pl.BlockSpec((mods, tile, columns), lambda i, *_: (level, i, 0))
    block = pl.BlockSpec((groups, tile, columns), lambda i, *_: (0, i, 0))
    anywhere = pl.BlockSpec(memory_space=pl.ANY)
    aliased = previous is not None
    whole = jax.ShapeDtypeStruct(anchor.shape, f32)
    return pl.pallas_call(
        functools.partial(update_kernel, groups, mods, aliased),
        grid_spec=pltpu.PrefetchScalarGridSpec(
            num_scalar_prefetch=2,
            grid=(rows // tile,),
            in_specs=[block, state, state] + ([anywhere, anywhere] if aliased else []),
            out_specs=[state, state, block],
            scratch_shapes=[pltpu.VMEM((mods, tile, columns), f32)],
        ),
        out_shape=[whole, whole, jax.ShapeDtypeStruct(received.shape, bf16)],
        input_output_aliases={5: 0, 6: 1} if aliased else {},
        compiler_params=params(),
        cost_estimate=pl.CostEstimate(
            flops=0,
            bytes_accessed=rows * columns * (groups * 4 + mods * 16),
            transcendentals=0,
        ),
    )(old, new, received, anchor, momentum, *(previous or ()))


OVER_ROWS = (((0,), (0,)), ((), ()))
OVER_COLUMNS = (((1,), (1,)), ((), ()))


def cost(flops, values, transcendentals=0):
    return pl.CostEstimate(flops=flops, bytes_accessed=values, transcendentals=transcendentals)


def norm_kernel(parts, depth, place, *refs):
    blocks = refs[:parts]
    out, scale = refs[parts : parts + 2]
    step = pl.program_id(1)

    @pl.when(step == 0)
    def _():
        total = jnp.zeros(scale.shape, f32)
        for block in blocks:
            values = block[...].astype(f32)
            total = total + jnp.sum(values * values, axis=-1, keepdims=True)
        scale[...] = lax.rsqrt(total / depth + epsilon)

    for at, block in enumerate(blocks):

        @pl.when(step == at)
        def _(block=block):
            out[...] = (block[...].astype(f32) * scale[...]).astype(out.dtype)


def normalize(own, parts, place):
    rows, width = own.shape
    depth = width * parts
    blocks = [own] + [lax.ppermute(own, "mp", around(parts, step)) for step in range(1, parts)]
    tile = min(256, rows)
    block = pl.BlockSpec((tile, width), lambda i, j, at: (i, 0))
    return pl.pallas_call(
        functools.partial(norm_kernel, parts, depth),
        grid_spec=pltpu.PrefetchScalarGridSpec(
            num_scalar_prefetch=1,
            grid=(rows // tile, parts),
            in_specs=[block] * parts,
            out_specs=[
                pl.BlockSpec(
                    (tile, width), lambda i, j, at: (i, lax.rem(at[0] + parts - j, parts))
                ),
                pl.BlockSpec((tile, 1), lambda i, j, at: (i, 0)),
            ],
        ),
        out_shape=[
            jax.ShapeDtypeStruct((rows, depth), bf16),
            jax.ShapeDtypeStruct((rows, 1), f32),
        ],
        compiler_params=params(),
        cost_estimate=cost(0, 4 * rows * depth),
    )(place.reshape(1).astype(jnp.int32), *blocks)


def grad_kernel(factor, normed, slope, out):
    product = lax.dot_general(normed[...], slope[...], OVER_ROWS, preferred_element_type=f32)
    out[...] = (product * factor).astype(out.dtype).reshape(out.shape)


def last_level_grad(normed, slope, factor, levels):
    rows, depth = normed.shape
    columns = slope.shape[1]
    tile = min(512, depth)
    return pl.pallas_call(
        functools.partial(grad_kernel, factor),
        grid=(depth // tile,),
        in_specs=[
            pl.BlockSpec((rows, tile), lambda i: (0, i)),
            pl.BlockSpec((rows, columns), lambda i: (0, 0)),
        ],
        out_specs=pl.BlockSpec((1, 1, tile, columns), lambda i: (0, levels - 1, i, 0)),
        out_shape=jax.ShapeDtypeStruct((1, levels, depth, columns), bf16),
        compiler_params=params(30),
        cost_estimate=cost(
            2 * rows * depth * columns, 2 * (rows * depth + rows * columns + depth * columns)
        ),
    )(normed, slope)


def state_kernel(factor, normed, weight, state, following, gate):
    pre = jnp.dot(normed[...], weight[...], preferred_element_type=f32) * factor
    sigmoid_part = jax.nn.sigmoid(pre)
    following[...] = (state[...].astype(f32) + pre * sigmoid_part).astype(bf16)
    gate[...] = sigmoid_part * (1.0 + pre * (1.0 - sigmoid_part))


def first_forward(normed, weight, state, factor):
    rows, depth = normed.shape
    columns = weight.shape[1]
    tile = min(256, rows)
    mine = pl.BlockSpec((tile, columns), lambda i: (i, 0))
    return pl.pallas_call(
        functools.partial(state_kernel, factor),
        grid=(rows // tile,),
        in_specs=[
            pl.BlockSpec((tile, depth), lambda i: (i, 0)),
            pl.BlockSpec((depth, columns), lambda i: (0, 0)),
            mine,
        ],
        out_specs=[mine, mine],
        out_shape=[
            jax.ShapeDtypeStruct((rows, columns), bf16),
            jax.ShapeDtypeStruct((rows, columns), f32),
        ],
        compiler_params=params(),
        cost_estimate=cost(
            2 * rows * depth * columns,
            2 * (rows * depth + 4 * rows * columns + depth * columns),
            rows * columns,
        ),
    )(normed, weight, state)


def slope_kernel(factor, width, at, normed, weight, upstream, slope, share, message):
    pre = jnp.dot(normed[...], weight[...], preferred_element_type=f32) * factor
    value = (upstream[...].astype(f32) * silu_slope(pre)).astype(bf16)
    slope[...] = value
    total = jnp.sum(value.astype(f32) * pre, axis=-1, keepdims=True)
    total = jnp.broadcast_to(total, (total.shape[0], 128)).T[: share.shape[0]]
    share[...] = total
    start = pl.multiple_of(at[0] * width, width)
    product = lax.dot_general(
        value, weight[pl.ds(start, width), :], OVER_COLUMNS, preferred_element_type=f32
    )
    height = value.shape[0]
    message[0, :height, :] = (product * factor).astype(message.dtype)
    high = total.astype(message.dtype)
    total = total - high.astype(f32)
    middle = total.astype(message.dtype)
    low = (total - middle.astype(f32)).astype(message.dtype)
    at = lax.broadcasted_iota(jnp.int32, total.shape, 0)
    pieces = jnp.where(at == 0, high.astype(f32), jnp.where(at == 1, middle.astype(f32), 0.0))
    pieces = jnp.where(at == 2, low.astype(f32), pieces)
    pieces = jnp.concatenate([pieces, jnp.zeros_like(pieces)], axis=0)
    message[0, height:, :] = pieces.astype(message.dtype)


def second_forward(normed, weight, upstream, where, width, factor):
    rows, depth = normed.shape
    columns = weight.shape[1]
    tile = width
    steps = rows // tile
    mine = pl.BlockSpec((tile, columns), lambda i, at: (i, 0))
    return pl.pallas_call(
        functools.partial(slope_kernel, factor, width),
        grid_spec=pltpu.PrefetchScalarGridSpec(
            num_scalar_prefetch=1,
            grid=(steps,),
            in_specs=[
                pl.BlockSpec((tile, depth), lambda i, at: (i, 0)),
                pl.BlockSpec((depth, columns), lambda i, at: (0, 0)),
                mine,
            ],
            out_specs=[
                mine,
                pl.BlockSpec((8, tile), lambda i, at: (0, i)),
                pl.BlockSpec((1, tile + 16, width), lambda i, at: (i, 0, 0)),
            ],
        ),
        out_shape=[
            jax.ShapeDtypeStruct((rows, columns), bf16),
            jax.ShapeDtypeStruct((8, rows), f32),
            jax.ShapeDtypeStruct((steps, tile + 16, width), bf16),
        ],
        compiler_params=params(),
        cost_estimate=cost(
            2 * rows * columns * (depth + width) // LIGHT,
            2 * (rows * (depth + 2 * columns) + depth * columns) // LIGHT,
        ),
    )(where.reshape(1).astype(jnp.int32), normed, weight, upstream)


def term_kernel(factor, where, slope, weight, out):
    product = lax.dot_general(slope[...], weight[...], OVER_COLUMNS, preferred_element_type=f32)
    out[...] = (product * factor).astype(out.dtype)


def term(slope, weight, where, width, factor):
    rows, columns = slope.shape
    tile = min(1024, rows)
    return pl.pallas_call(
        functools.partial(term_kernel, factor),
        grid_spec=pltpu.PrefetchScalarGridSpec(
            num_scalar_prefetch=1,
            grid=(rows // tile,),
            in_specs=[
                pl.BlockSpec((tile, columns), lambda i, at: (i, 0)),
                pl.BlockSpec((width, columns), lambda i, at: (at[0], 0)),
            ],
            out_specs=pl.BlockSpec((tile, width), lambda i, at: (i, 0)),
        ),
        out_shape=jax.ShapeDtypeStruct((rows, width), bf16),
        compiler_params=params(30),
        cost_estimate=cost(
            2 * rows * columns * width // LIGHT,
            2 * (rows * columns + columns * width + rows * width) // LIGHT,
        ),
    )(where.reshape(1).astype(jnp.int32), slope, weight)


def first_kernel(factor, runs, *refs):
    normed, scale, share, upstream, state, gate, kept = refs[:7]
    terms = refs[7:-4]
    out, slope, total = refs[-3:]
    tile, columns = slope.shape
    width = columns // runs
    count = len(terms) // runs
    step = pl.program_id(0)
    last = pl.num_programs(0) - 1
    for run in range(runs):
        here = slice(run * width, (run + 1) * width)
        normed_grad = kept[:, here].astype(f32)
        for other in terms[run * count : (run + 1) * count]:
            arrived = other[0, :tile, :] if len(other.shape) == 3 else other[...]
            normed_grad = normed_grad + arrived.astype(f32)
        state_grad = (
            upstream[:, here].astype(f32)
            + scale[...] * normed_grad
            - state[:, here].astype(f32) * share[...]
        )
        slope[:, here] = (state_grad * gate[:, here]).astype(bf16)
    product = lax.dot_general(normed[...], slope[...], OVER_ROWS, preferred_element_type=f32)

    @pl.when(step == 0)
    def _():
        total[...] = product

    @pl.when(jnp.logical_and(step > 0, step < last))
    def _():
        total[...] = total[...] + product

    @pl.when(step == last)
    def _():
        whole = jnp.where(step > 0, total[...] + product, product)
        out[...] = (whole * factor).astype(out.dtype).reshape(out.shape)


def first_level_grad(normed, scale, share, mine, terms, runs, block, width, tile, factor, grads):
    rows, depth = normed.shape
    columns = runs * width
    column = pl.BlockSpec((tile, 1), lambda i: (i, 0))
    part = pl.BlockSpec((tile, columns), lambda i: (i, block))
    message = pl.BlockSpec((1, tile + 16, width), lambda i: (i, 0, 0))
    plain = pl.BlockSpec((tile, width), lambda i: (i, 0))
    return pl.pallas_call(
        functools.partial(first_kernel, factor, runs),
        grid=(rows // tile,),
        in_specs=[pl.BlockSpec((tile, depth), lambda i: (i, 0)), column, column]
        + [part] * len(mine)
        + [message if value.ndim == 3 else plain for value in terms]
        + [pl.BlockSpec(memory_space=pl.ANY)],
        out_specs=pl.BlockSpec((1, 1, depth, columns), lambda i: (0, 0, 0, block)),
        out_shape=jax.ShapeDtypeStruct(grads.shape, bf16),
        scratch_shapes=[pltpu.VMEM((tile, columns), bf16), pltpu.VMEM((depth, columns), f32)],
        input_output_aliases={3 + len(mine) + len(terms): 0},
        compiler_params=params(44),
        cost_estimate=cost(
            2 * rows * depth * columns * HEAVY,
            2 * (rows * depth + 7 * rows * columns + depth * columns) * HEAVY,
        ),
    )(normed, scale, share, *mine, *terms, grads)


def around(parts, step):
    return [(p, (p + step) % parts) for p in range(parts)]


def after(value, *others):
    return lax.optimization_barrier((value, *others))[0]


def shards(anchor, momentum, deltas, old_path, new_path, tokens, cotangent):
    groups = lax.axis_size("group")
    parts = lax.axis_size("mp")
    place = lax.axis_index("mp")
    levels = deltas.shape[1]
    depth = deltas.shape[2]
    columns = deltas.shape[3]
    factor = 1.0 / math.sqrt(depth)

    def exchange(blocks):
        return lax.all_to_all(blocks, "group", split_axis=0, concat_axis=0, tiled=True)

    received = [exchange(cast_level(deltas, level, groups)) for level in range(levels)]
    first_normed, _ = normalize(tokens[0], parts, place)
    received[0] = after(received[0], first_normed)

    previous = None
    loaded = []
    for level in range(levels):
        part_anchor, part_momentum, outgoing = outer_update(
            received[level],
            anchor,
            momentum,
            old_path[:, level],
            new_path[:, level],
            level,
            levels,
            previous,
        )
        previous = (part_anchor, part_momentum)
        loaded.append(exchange(outgoing).reshape(depth, columns))
    new_anchor, new_momentum = previous
    first_weight, second_weight = loaded

    upstream = cotangent[0]
    second_state, gate = first_forward(first_normed, first_weight, tokens[0], factor)
    second_normed, second_scale = normalize(second_state, parts, place)

    own_features = depth // parts
    width = min(RUN, own_features)
    runs = own_features // width

    def place_of(step, run):
        return lax.rem(place + step, parts) * runs + run

    def send(values):
        return [lax.ppermute(values[n], "mp", around(parts, n + 1)) for n in range(len(values))]

    def terms_of(source, run, steps):
        return [
            term(source, second_weight, place_of(step, run), width, factor) for step in steps
        ]

    rows = second_normed.shape[0]
    slope, own_share, message = second_forward(
        second_normed, second_weight, upstream, place_of(1, 0), width, factor
    )
    message = lax.ppermute(message, "mp", around(parts, 1))
    share = own_share[0] + jnp.sum(message[:, width : width + 3].astype(f32), axis=1).reshape(-1)
    arrived = [[message]]
    for step in range(2, parts):
        share = share + lax.ppermute(own_share, "mp", around(parts, step))[0]
        [value] = terms_of(slope, 0, [step])
        arrived[0].append(lax.ppermute(value, "mp", around(parts, step)))
    source = slope
    kept = grads = None
    for run in range(1, runs + 2):
        if run < runs:
            sent = terms_of(source, run, range(1, parts))
            arrived.append(send(sent))
            source = after(slope, sent[0])
        if kept is None:
            kept = term(source, second_weight, place, own_features, factor)
            source = after(slope, kept)
        elif grads is None:
            grads = last_level_grad(second_normed, source, factor, levels)
            source = after(slope, grads)
        if run < runs:
            source = after(source, *arrived[run - 1])
    scaled = second_scale**2 * after(share, grads).reshape(rows, 1) / depth
    mine = [upstream, second_state, gate, kept]
    bounds = [0] + list(range(max(1, runs - 2), runs + 1))
    for begin, end in zip(bounds[:-1], bounds[1:]):
        terms = [value for run in range(begin, end) for value in arrived[run]]
        grads = first_level_grad(
            first_normed,
            second_scale,
            scaled,
            mine,
            terms,
            end - begin,
            begin // (end - begin),
            width,
            width,
            factor,
            grads,
        )
    return (new_anchor, new_momentum, grads)


def solution(mesh):
    in_specs = (
        P(None, "group", "mp"),
        P(None, "group", "mp"),
        P("group", None, None, "mp"),
        P(),
        P(),
        P("group", None, "mp"),
        P("group", None, "mp"),
    )
    out_specs = (P(None, "group", "mp"), P(None, "group", "mp"), P("group", None, None, "mp"))
    return jax.shard_map(shards, mesh=mesh, in_specs=in_specs, out_specs=out_specs, check_vma=False)
```
